256 devices in a mesh: row: 16 (over z_hi, x), col: 16 (over z_lo, y, core).
Axes of the slice: x: 4, y: 4, z: 8 (z_hi: 4, z_lo: 2; z = z_hi * 2 + z_lo), core: 2. Of those that a mesh axis runs over, the one named last changes fastest.
Arguments:
- features: bfloat16 [131072, 8192], P(('row', 'col')), may hold values from -18 to 18
- prior: float32 [512], replicated, may hold values from 32768 to 524288
Outputs:
- panel_rows: float32 [16, 512, 512], P('row')
- trailing_update: float32 [16, 512, 16, 512], P('row', None, 'col')
The draws below stay inside these ranges and needn't reach their ends.
All inputs are finite; a program needn't handle non-finite values.
Results may differ from the reference program's by a relative error of at most 0.0054.
Values may be sent and summed in bfloat16 or wider, within the bound.
A program may use at most 128 MiB of HBM per device.

```python
import math
import jax
import jax.numpy as jnp
from jax import lax

W = 8192
BLOCK = 256
PANEL = 512
TOKENS = 131072
N_ROW = 16
N_COL = 16


def draw_features(key, part):
    key = jax.random.fold_in(key, 11)
    first, second = jax.random.split(key, 2)
    scales = jnp.exp(jax.random.uniform(first, (W,), jnp.float32, jnp.log(0.5), jnp.log(2.0)))
    values = jnp.clip(jax.random.normal(second, (TOKENS, W), jnp.float32), -5.0, 5.0) * scales[None, :]
    return values.astype(jnp.bfloat16)


def setup_inputs(seed: int = 0) -> dict:
    arg_keys = jax.random.split(jax.random.key(seed), 3)
    features = draw_features(jax.random.fold_in(arg_keys[2], 71), 0)
    prior = jnp.clip(jnp.exp(jax.random.uniform(arg_keys[1], (PANEL,), jnp.float32, math.log(32768.0), math.log(524288.0))), 32768.0, 524288.0)
    return dict(features=features, prior=prior)


def inverse_factor(tile):
    lower = jnp.linalg.cholesky(tile)
    return jax.scipy.linalg.solve_triangular(lower, jnp.eye(tile.shape[0], dtype=jnp.float32), lower=True)

def owner_order(matrix, groups):
    cycles = W // (BLOCK * groups)
    return matrix.reshape(cycles, groups, BLOCK, matrix.shape[1]).transpose(1, 0, 2, 3).reshape(W, matrix.shape[1])

def reference(features, prior):
    highest = lax.Precision.HIGHEST
    gram = lax.dot_general(features.astype(jnp.float32), features[:, :PANEL].astype(jnp.float32), (((0,), (0,)), ((), ())), preferred_element_type=jnp.float32)
    gram = gram + jnp.concatenate([jnp.diag(prior), jnp.zeros((W - PANEL, PANEL), jnp.float32)], 0)
    inv_first = inverse_factor(gram[:BLOCK, :BLOCK])
    first = jnp.dot(gram[:, :BLOCK].astype(jnp.float32), inv_first.T.astype(jnp.float32), precision=highest, preferred_element_type=jnp.float32)
    lead = first[BLOCK:PANEL]
    rest = gram[:, BLOCK:] - jnp.dot(first.astype(jnp.float32), lead.T.astype(jnp.float32), precision=highest, preferred_element_type=jnp.float32)
    inv_second = inverse_factor(rest[BLOCK:PANEL])
    second = jnp.dot(rest.astype(jnp.float32), inv_second.T.astype(jnp.float32), precision=highest, preferred_element_type=jnp.float32)
    second = jnp.where(jnp.arange(W)[:, None] >= BLOCK, second, jnp.zeros_like(second))
    panel = jnp.concatenate([first, second], 1)
    panel_rows = owner_order(panel, N_ROW).reshape(N_ROW, W // N_ROW, PANEL)
    rounded = panel.astype(jnp.bfloat16)
    row_side = owner_order(rounded, N_ROW)
    col_side = owner_order(rounded, N_COL)
    update = jnp.dot(row_side.astype(jnp.float32), col_side.T.astype(jnp.float32), preferred_element_type=jnp.float32) / PANEL
    return (panel_rows, update.reshape(N_ROW, W // N_ROW, N_COL, W // N_COL))
```

```python
import jax
import jax.numpy as jnp
from jax import lax
from jax.experimental import pallas as pl
from jax.experimental.pallas import tpu as pltpu
from jax.sharding import PartitionSpec as P

W = 8192
BLOCK = 256
PANEL = 512
TOKENS = 512
HALF = W // 2
MESH = pl.DeviceIdType.MESH
WIRE = jnp.bfloat16
F32 = jnp.float32
ORDERS = (
    ("xa", "xb", "ya", "yb"),
    ("xb", "ya", "yb", "xa"),
    ("ya", "yb", "xa", "xb"),
    ("yb", "xa", "xb", "ya"),
)
FULL = slice(None)


class Place:
    def __init__(self):
        self.r = lax.axis_index("row")
        self.c = lax.axis_index("col")
        self.x = self.r % 4
        self.y = (self.c // 2) % 4
        self.zh = self.r // 4
        self.zl = self.c // 8
        self.z = self.zh * 2 + self.zl
        self.core = self.c % 2
        self.bits = {
            "xa": ((self.x + 1) // 2) % 2,
            "xb": self.x // 2,
            "ya": ((self.y + 1) // 2) % 2,
            "yb": self.y // 2,
        }

    def at(self, x=None, y=None, z=None, core=None):
        x = self.x if x is None else x
        y = self.y if y is None else y
        z = self.z if z is None else z
        core = self.core if core is None else core
        return (z // 2 * 4 + x, z % 2 * 8 + y * 2 + core)

    def partner(self, dim):
        if dim == "xa":
            return self.at(x=self.x + 1 - 2 * (self.x % 2))
        if dim == "xb":
            return self.at(x=3 - self.x)
        if dim == "ya":
            return self.at(y=self.y + 1 - 2 * (self.y % 2))
        return self.at(y=3 - self.y)


def tile_index(place, quarter, zh, step, last):
    fixed = {}
    for k, dim in enumerate(ORDERS[quarter][: step + 1]):
        mine = place.bits[dim]
        fixed[dim] = mine if (k < step or last) else 1 - mine
    pick = lambda dim: fixed.get(dim, FULL)
    return (zh, pick("xb"), pick("xa"), quarter, pick("ya"), pick("yb"))


def top_index(place, quarter, step, last):
    _, xb, xa, _, ya, yb = tile_index(place, quarter, 0, step, last)
    return (quarter, ya, yb, xb, xa)


def gather_kernel(feat, rows_out, top_out, own, theirs, lead_own, lead_their, lead_t, acc, top,
                  s0, s1, s2, s3, r0, r1, r2, r3, ts0, ts1, ts2, ts3, tr0, tr1, tr2, tr3,
                  zsend, zrecv, zown, topz,
                  load_sem, feat_send, feat_recv, step_send, step_recv, top_send, top_recv,
                  z_send, z_recv, tz_send, tz_recv, tg_send, tg_recv, core_send, core_recv,
                  row_send, row_recv, col_send, col_recv):
    me = Place()
    sends, recvs = (s0, s1, s2, s3), (r0, r1, r2, r3)
    tsends, trecvs = (ts0, ts1, ts2, ts3), (tr0, tr1, tr2, tr3)
    mate = me.at(core=1 - me.core)
    loads = [pltpu.make_async_copy(feat.at[:, pl.ds(0, PANEL)], lead_own, load_sem.at[0])]
    for i in range(4):
        loads.append(
            pltpu.make_async_copy(
                feat.at[:, pl.ds(pl.multiple_of(me.core * HALF + i * 1024, 1024), 1024)],
                own.at[:, pl.ds(i * 1024, 1024)],
                load_sem.at[i + 1],
            )
        )
    for load in loads:
        load.start()

    barrier = pltpu.get_barrier_semaphore()

    def greet(device):
        pl.semaphore_signal(barrier, inc=1, device_id=device, device_id_type=MESH)

    greet(mate)
    for dim in ORDERS[0]:
        greet(me.partner(dim))
    for j in range(1, 8):
        greet(me.at(z=(me.z + j) % 8))
    pl.semaphore_wait(barrier, 12)

    shares = [
        pltpu.make_async_remote_copy(
            src_ref=feat.at[:, pl.ds(0, PANEL)], dst_ref=lead_their,
            send_sem=feat_send.at[0], recv_sem=feat_recv.at[0],
            device_id=mate, device_id_type=MESH,
        )
    ]
    for i in range(4):
        shares.append(
            pltpu.make_async_remote_copy(
                src_ref=feat.at[:, pl.ds(pl.multiple_of((1 - me.core) * HALF + i * 1024, 1024), 1024)],
                dst_ref=theirs.at[:, pl.ds(i * 1024, 1024)],
                send_sem=feat_send.at[i + 1], recv_sem=feat_recv.at[i + 1],
                device_id=mate, device_id_type=MESH,
            )
        )
    for share in shares:
        share.start()

    loads[0].wait()
    lead_t[:, :TOKENS] = lead_own[...].T
    shares[0].wait_recv()
    lead_t[:, TOKENS:] = lead_their[...].T

    def products(left, right):
        return jnp.dot(lead_t[:, :TOKENS], left, preferred_element_type=F32) + jnp.dot(
            lead_t[:, TOKENS:], right, preferred_element_type=F32
        )

    lanes = pl.ds(pl.multiple_of(me.core * BLOCK, BLOCK), BLOCK)
    top[...] = products(lead_own[:, lanes], lead_their[:, lanes]).reshape(4, 2, 2, 2, 2, 8, BLOCK)

    def exchange(src, dst, send, recv, device):
        return pltpu.make_async_remote_copy(
            src_ref=src, dst_ref=dst, send_sem=send, recv_sem=recv,
            device_id=device, device_id_type=MESH,
        )

    def top_copy(step, q):
        return exchange(
            tsends[step].at[q], trecvs[step].at[q], top_send.at[step, q], top_recv.at[step, q],
            me.partner(ORDERS[q][step]),
        )

    def top_start(step):
        for q in range(4):
            tsends[step][q] = top[top_index(me, q, step, False)]
            top_copy(step, q).start()

    def top_finish(step):
        for q in range(4):
            top_copy(step, q).wait_recv()
            at = top_index(me, q, step, True)
            top[at] = top[at] + trecvs[step][q]

    def main_copy(step, zh, q):
        return exchange(
            sends[step].at[zh, q], recvs[step].at[zh, q],
            step_send.at[step, zh, q], step_recv.at[step, zh, q],
            me.partner(ORDERS[q][step]),
        )

    def main_start(step, zh):
        for q in range(4):
            sends[step][zh, q] = acc[tile_index(me, q, zh, step, False)].astype(WIRE)
            main_copy(step, zh, q).start()

    def main_finish(step, zh):
        for q in range(4):
            main_copy(step, zh, q).wait_recv()
            at = tile_index(me, q, zh, step, True)
            acc[at] = acc[at] + recvs[step][zh, q].astype(F32)

    def multiply(zh):
        loads[zh + 1].wait()
        shares[zh + 1].wait_recv()

        def body(p, carry):
            xb, xa = p // 2, p % 2
            x = 2 * xb + (xb + xa) % 2
            at = pl.ds(pl.multiple_of((zh * 4 + x) * BLOCK, BLOCK), BLOCK)
            acc[zh, xb, xa] = products(own[:, at], theirs[:, at]).reshape(4, 2, 2, 32, BLOCK)
            return carry

        lax.fori_loop(0, 4, body, 0)

    my_top = (me.bits["ya"], me.bits["yb"], me.bits["xb"], me.bits["xa"])
    my_slot = 8 * my_top[0] + 4 * my_top[1] + 2 * my_top[2] + my_top[3]
    top_start(0)
    for wave in range(8):
        if wave >= 1 and wave <= 4:
            top_finish(wave - 1)
            if wave < 4:
                top_start(wave)
            else:
                for q in range(4):
                    topz[me.z, q] = top[(q,) + my_top]
                top_plane = [
                    exchange(topz.at[me.z], topz.at[me.z], tz_send.at[j - 1], tz_recv,
                             me.at(z=(me.z + j) % 8))
                    for j in range(1, 8)
                ]
                for copy in top_plane:
                    copy.start()
        if wave < 4:
            multiply(wave)
            main_start(0, wave)
        if wave == 5:
            pltpu.make_async_copy(topz.at[pl.ds(0, 7)], topz.at[pl.ds(0, 7)], tz_recv).wait()
            for q in range(4):
                total = topz[0, q]
                for z in range(1, 8):
                    total = total + topz[z, q]
                top_out[me.core, my_slot, q] = total
            top_gather = [
                exchange(top_out.at[me.core, my_slot], top_out.at[me.core, my_slot],
                         tg_send.at[j - 1], tg_recv,
                         me.at(x=(me.x + j) % 4, y=(me.y + j // 4) % 4))
                for j in range(1, 16)
            ]
            for copy in top_gather:
                copy.start()
        for step in range(4):
            zh = wave - step - 1
            if 0 <= zh < 4:
                main_finish(step, zh)
                if step < 3:
                    main_start(step + 1, zh)
        if wave == 6:
            fifteen = top_out.at[me.core, pl.ds(0, 15)]
            pltpu.make_async_copy(fifteen, fifteen, tg_recv).wait()
            top_mate = exchange(top_out.at[me.core], top_out.at[me.core], core_send, core_recv, mate)
            top_mate.start()

    home = lambda q, zh: (zh, me.bits["xb"], me.bits["xa"], q, me.bits["ya"], me.bits["yb"])
    for q in range(4):
        for zh in range(4):
            tile = acc[home(q, zh)]
            for zl in range(2):
                zsend[zh * 2 + zl, q] = tile[:, zl * 128 : zl * 128 + 128].astype(WIRE)
        tile = acc[home(q, me.zh)]
        for zl in range(2):
            zown[zl, q] = tile[:, zl * 128 : zl * 128 + 128]
    plane = [
        exchange(zsend.at[(me.z + j) % 8], zrecv.at[me.z], z_send.at[j - 1], z_recv,
                 me.at(z=(me.z + j) % 8))
        for j in range(1, 8)
    ]
    for copy in plane:
        copy.start()
    pltpu.make_async_copy(zrecv.at[pl.ds(0, 7)], zrecv.at[pl.ds(0, 7)], z_recv).wait()
    slot = 8 * me.core + 4 * me.zl + 2 * me.bits["ya"] + me.bits["yb"]
    for q in range(4):
        total = zown[me.zl, q]
        for j in range(1, 8):
            total = total + zrecv[(me.z + j) % 8, q].astype(F32)
        rows_out[0, slot, q] = total.astype(rows_out.dtype)
    mine = rows_out.at[0, slot]
    row_copies = [
        exchange(mine, mine, row_send.at[j - 1], row_recv, (me.r, (me.c + j) % 16))
        for j in range(1, 16)
    ]
    col_copies = [
        exchange(mine, rows_out.at[1, slot], col_send.at[j], col_recv, ((me.r + j) % 16, me.r))
        for j in range(16)
    ]
    for j in range(1, 16):
        col_copies[j].start()
        row_copies[j - 1].start()

    @pl.when(me.r != me.c)
    def _():
        col_copies[0].start()

    @pl.when(me.r == me.c)
    def _():
        rows_out[1, slot] = rows_out[0, slot]

    top_mate.wait()
    fifteen = rows_out.at[0, pl.ds(0, 15)]
    pltpu.make_async_copy(fifteen, fifteen, row_recv).wait()

    @pl.when(me.r != me.c)
    def _():
        pltpu.make_async_copy(rows_out.at[1], rows_out.at[1], col_recv).wait()
        col_copies[0].wait_send()

    @pl.when(me.r == me.c)
    def _():
        pltpu.make_async_copy(fifteen, fifteen, col_recv).wait()

    for copies in (row_copies, col_copies[1:], plane, top_plane, top_gather, shares):
        for copy in copies:
            copy.wait_send()
    for step in range(4):
        for q in range(4):
            top_copy(step, q).wait_send()
            for zh in range(4):
                main_copy(step, zh, q).wait_send()


def gather_rows(features):
    twos = lambda n: (2,) * n
    wire = lambda n: pltpu.VMEM((4, 4) + twos(n) + (32, BLOCK), WIRE)
    exact = lambda n: pltpu.VMEM((4,) + twos(n) + (8, BLOCK), F32)
    dma = pltpu.SemaphoreType.DMA
    return pl.pallas_call(
        gather_kernel,
        out_shape=(
            jax.ShapeDtypeStruct((2, 16, 4, 32, 128), WIRE),
            jax.ShapeDtypeStruct((2, 16, 4, 8, BLOCK), F32),
        ),
        in_specs=[pl.BlockSpec(memory_space=pl.ANY)],
        out_specs=(pl.BlockSpec(memory_space=pltpu.VMEM),) * 2,
        scratch_shapes=[
            pltpu.VMEM((TOKENS, HALF), jnp.bfloat16),
            pltpu.VMEM((TOKENS, HALF), jnp.bfloat16),
            pltpu.VMEM((TOKENS, PANEL), jnp.bfloat16),
            pltpu.VMEM((TOKENS, PANEL), jnp.bfloat16),
            pltpu.VMEM((PANEL, 2 * TOKENS), jnp.bfloat16),
            pltpu.VMEM((4, 2, 2, 4, 2, 2, 32, BLOCK), F32),
            pltpu.VMEM((4, 2, 2, 2, 2, 8, BLOCK), F32),
            *[wire(n) for n in (3, 2, 1, 0)],
            *[wire(n) for n in (3, 2, 1, 0)],
            *[exact(n) for n in (3, 2, 1, 0)],
            *[exact(n) for n in (3, 2, 1, 0)],
            pltpu.VMEM((8, 4, 32, 128), WIRE),
            pltpu.VMEM((8, 4, 32, 128), WIRE),
            pltpu.VMEM((2, 4, 32, 128), F32),
            pltpu.VMEM((8, 4, 8, BLOCK), F32),
            dma((5,)), dma((5,)), dma((5,)),
            dma((4, 4, 4)), dma((4, 4, 4)), dma((4, 4)), dma((4, 4)),
            dma((7,)), dma, dma((7,)), dma, dma((15,)), dma, dma, dma,
            dma((15,)), dma, dma((16,)), dma,
        ],
        compiler_params=pltpu.CompilerParams(
            collective_id=1, has_side_effects=True, vmem_limit_bytes=56 * 2**20
        ),
        cost_estimate=pl.CostEstimate(
            flops=2 * PANEL * 1024 * HALF, bytes_accessed=10 * 2**20, transcendentals=0
        ),
        name="reduce_gram",
    )(features)


def inverse_factor(tile):
    lower = jnp.linalg.cholesky(tile)
    return jax.scipy.linalg.solve_triangular(
        lower, jnp.eye(tile.shape[0], dtype=jnp.float32), lower=True
    )


def dot(left, right):
    return jnp.dot(left, right, precision=lax.Precision.HIGHEST, preferred_element_type=F32)


def on_device(features, prior):
    r, c = lax.axis_index("row"), lax.axis_index("col")
    rows, top = gather_rows(features)
    top = top.transpose(2, 1, 3, 0, 4).reshape(PANEL, PANEL) + jnp.diag(prior)
    gram = rows.astype(F32).reshape(2, 2, 2, 4, 4, 32, 128).transpose(0, 4, 3, 5, 1, 2, 6).reshape(2, PANEL, PANEL)
    own = jnp.stack([r, c])
    exact = jnp.where((own == 0)[:, None, None], top[None, :, :BLOCK], top[None, :, BLOCK:])
    gram = gram.at[:, :, :BLOCK].set(
        jnp.where((own < 2)[:, None, None], exact, gram[:, :, :BLOCK])
    )
    gram = gram.transpose(1, 0, 2).reshape(PANEL, 2 * PANEL)
    inv_first = inverse_factor(top[:BLOCK, :BLOCK])
    lead = dot(top[BLOCK:, :BLOCK], inv_first.T)
    inv_second = inverse_factor(top[BLOCK:, BLOCK:] - dot(lead, lead.T))
    first = dot(inv_first, gram[:BLOCK])
    second = dot(inv_second, gram[BLOCK:] - dot(lead, first))
    second = second.reshape(BLOCK, 2, PANEL)
    dead = (own == 0)[None, :, None] & (lax.iota(jnp.int32, PANEL) < BLOCK)[None, None, :]
    second = jnp.where(dead, 0.0, second)
    panel = jnp.concatenate([first.reshape(BLOCK, 2, PANEL), second], 0)
    rounded = panel.astype(jnp.bfloat16)
    update = (
        lax.dot_general(
            rounded[:, 0], rounded[:, 1], (((0,), (0,)), ((), ())), preferred_element_type=F32
        )
        / PANEL
    )
    return (panel[:, 0].T[None], update[None, :, None, :])


def solution(mesh):
    placed = (P(("row", "col"), None), P())
    return jax.shard_map(
        on_device,
        mesh=mesh,
        in_specs=placed,
        out_specs=(P("row", None, None), P("row", None, "col", None)),
        check_vma=False,
    )
```

```python
import jax
import jax.numpy as jnp
from jax import lax
from jax.experimental import pallas as pl
from jax.experimental.pallas import tpu as pltpu
from jax.sharding import PartitionSpec as P

W = 8192
BLOCK = 256
PANEL = 512
TOKENS = 512
HALF = W // 2
MESH = pl.DeviceIdType.MESH
WIRE = jnp.bfloat16
F32 = jnp.float32
ORDERS = (
    ("xa", "xb", "ya", "yb"),
    ("xb", "ya", "yb", "xa"),
    ("ya", "yb", "xa", "xb"),
    ("yb", "xa", "xb", "ya"),
)
FULL = slice(None)


class Place:
    def __init__(self):
        self.r = lax.axis_index("row")
        self.c = lax.axis_index("col")
        self.x = self.r % 4
        self.y = (self.c // 2) % 4
        self.zh = self.r // 4
        self.zl = self.c // 8
        self.z = self.zh * 2 + self.zl
        self.core = self.c % 2
        self.bits = {
            "xa": ((self.x + 1) // 2) % 2,
            "xb": self.x // 2,
            "ya": ((self.y + 1) // 2) % 2,
            "yb": self.y // 2,
        }

    def at(self, x=None, y=None, z=None, core=None):
        x = self.x if x is None else x
        y = self.y if y is None else y
        z = self.z if z is None else z
        core = self.core if core is None else core
        return (z // 2 * 4 + x, z % 2 * 8 + y * 2 + core)

    def partner(self, dim):
        if dim == "xa":
            return self.at(x=self.x + 1 - 2 * (self.x % 2))
        if dim == "xb":
            return self.at(x=3 - self.x)
        if dim == "ya":
            return self.at(y=self.y + 1 - 2 * (self.y % 2))
        return self.at(y=3 - self.y)


def tile_index(place, quarter, zh, step, last):
    fixed = {}
    for k, dim in enumerate(ORDERS[quarter][: step + 1]):
        mine = place.bits[dim]
        fixed[dim] = mine if (k < step or last) else 1 - mine
    pick = lambda dim: fixed.get(dim, FULL)
    return (zh, pick("xb"), pick("xa"), quarter, pick("ya"), pick("yb"))


def top_index(place, quarter, step, last):
    _, xb, xa, _, ya, yb = tile_index(place, quarter, 0, step, last)
    return (quarter, ya, yb, xb, xa)


def gather_kernel(feat, rows_out, top_out, own, theirs, lead_own, lead_their, lead_t, acc, top,
                  s0, s1, s2, s3, r0, r1, r2, r3, ts0, ts1, ts2, ts3, tr0, tr1, tr2, tr3,
                  zsend, zrecv, zown, topz,
                  load_sem, feat_send, feat_recv, step_send, step_recv, top_send, top_recv,
                  z_send, z_recv, tz_send, tz_recv, tg_send, tg_recv, core_send, core_recv,
                  row_send, row_recv, col_send, col_recv):
    me = Place()
    sends, recvs = (s0, s1, s2, s3), (r0, r1, r2, r3)
    tsends, trecvs = (ts0, ts1, ts2, ts3), (tr0, tr1, tr2, tr3)
    mate = me.at(core=1 - me.core)
    loads = [pltpu.make_async_copy(feat.at[:, pl.ds(0, PANEL)], lead_own, load_sem.at[0])]
    for i in range(4):
        loads.append(
            pltpu.make_async_copy(
                feat.at[:, pl.ds(pl.multiple_of(me.core * HALF + i * 1024, 1024), 1024)],
                own.at[:, pl.ds(i * 1024, 1024)],
                load_sem.at[i + 1],
            )
        )
    for load in loads:
        load.start()

    barrier = pltpu.get_barrier_semaphore()

    def greet(device):
        pl.semaphore_signal(barrier, inc=1, device_id=device, device_id_type=MESH)

    greet(mate)
    for dim in ORDERS[0]:
        greet(me.partner(dim))
    for j in range(1, 8):
        greet(me.at(z=(me.z + j) % 8))
    pl.semaphore_wait(barrier, 12)

    shares = [
        pltpu.make_async_remote_copy(
            src_ref=feat.at[:, pl.ds(0, PANEL)], dst_ref=lead_their,
            send_sem=feat_send.at[0], recv_sem=feat_recv.at[0],
            device_id=mate, device_id_type=MESH,
        )
    ]
    for i in range(4):
        shares.append(
            pltpu.make_async_remote_copy(
                src_ref=feat.at[:, pl.ds(pl.multiple_of((1 - me.core) * HALF + i * 1024, 1024), 1024)],
                dst_ref=theirs.at[:, pl.ds(i * 1024, 1024)],
                send_sem=feat_send.at[i + 1], recv_sem=feat_recv.at[i + 1],
                device_id=mate, device_id_type=MESH,
            )
        )
    for share in shares:
        share.start()

    loads[0].wait()
    lead_t[:, :TOKENS] = lead_own[...].T
    shares[0].wait_recv()
    lead_t[:, TOKENS:] = lead_their[...].T

    def products(left, right):
        return jnp.dot(lead_t[:, :TOKENS], left, preferred_element_type=F32) + jnp.dot(
            lead_t[:, TOKENS:], right, preferred_element_type=F32
        )

    lanes = pl.ds(pl.multiple_of(me.core * BLOCK, BLOCK), BLOCK)
    top[...] = products(lead_own[:, lanes], lead_their[:, lanes]).reshape(4, 2, 2, 2, 2, 8, BLOCK)

    def exchange(src, dst, send, recv, device):
        return pltpu.make_async_remote_copy(
            src_ref=src, dst_ref=dst, send_sem=send, recv_sem=recv,
            device_id=device, device_id_type=MESH,
        )

    def top_copy(step, q):
        return exchange(
            tsends[step].at[q], trecvs[step].at[q], top_send.at[step, q], top_recv.at[step, q],
            me.partner(ORDERS[q][step]),
        )

    def top_start(step):
        for q in range(4):
            tsends[step][q] = top[top_index(me, q, step, False)]
            top_copy(step, q).start()

    def top_finish(step):
        for q in range(4):
            top_copy(step, q).wait_recv()
            at = top_index(me, q, step, True)
            top[at] = top[at] + trecvs[step][q]

    def main_copy(step, zh, q):
        return exchange(
            sends[step].at[zh, q], recvs[step].at[zh, q],
            step_send.at[step, zh, q], step_recv.at[step, zh, q],
            me.partner(ORDERS[q][step]),
        )

    def main_start(step, zh):
        for q in range(4):
            sends[step][zh, q] = acc[tile_index(me, q, zh, step, False)].astype(WIRE)
            main_copy(step, zh, q).start()

    def main_finish(step, zh):
        for q in range(4):
            main_copy(step, zh, q).wait_recv()
            at = tile_index(me, q, zh, step, True)
            acc[at] = acc[at] + recvs[step][zh, q].astype(F32)

    def multiply(zh):
        loads[zh + 1].wait()
        shares[zh + 1].wait_recv()

        def body(p, carry):
            xb, xa = p // 2, p % 2
            x = 2 * xb + (xb + xa) % 2
            at = pl.ds(pl.multiple_of((zh * 4 + x) * BLOCK, BLOCK), BLOCK)
            acc[zh, xb, xa] = products(own[:, at], theirs[:, at]).reshape(4, 2, 2, 32, BLOCK)
            return carry

        lax.fori_loop(0, 4, body, 0)

    my_top = (me.bits["ya"], me.bits["yb"], me.bits["xb"], me.bits["xa"])
    my_slot = 8 * my_top[0] + 4 * my_top[1] + 2 * my_top[2] + my_top[3]
    top_start(0)
    for wave in range(8):
        if wave >= 1 and wave <= 4:
            top_finish(wave - 1)
            if wave < 4:
                top_start(wave)
            else:
                for q in range(4):
                    topz[me.z, q] = top[(q,) + my_top]
                top_plane = [
                    exchange(topz.at[me.z], topz.at[me.z], tz_send.at[j - 1], tz_recv,
                             me.at(z=(me.z + j) % 8))
                    for j in range(1, 8)
                ]
                for copy in top_plane:
                    copy.start()
        if wave < 4:
            multiply(wave)
            main_start(0, wave)
        if wave == 5:
            pltpu.make_async_copy(topz.at[pl.ds(0, 7)], topz.at[pl.ds(0, 7)], tz_recv).wait()
            for q in range(4):
                total = topz[0, q]
                for z in range(1, 8):
                    total = total + topz[z, q]
                top_out[me.core, my_slot, q] = total
            top_gather = [
                exchange(top_out.at[me.core, my_slot], top_out.at[me.core, my_slot],
                         tg_send.at[j - 1], tg_recv,
                         me.at(x=(me.x + j) % 4, y=(me.y + j // 4) % 4))
                for j in range(1, 16)
            ]
            for copy in top_gather:
                copy.start()
        for step in range(4):
            zh = wave - step - 1
            if 0 <= zh < 4:
                main_finish(step, zh)
                if step < 3:
                    main_start(step + 1, zh)
        if wave == 6:
            fifteen = top_out.at[me.core, pl.ds(0, 15)]
            pltpu.make_async_copy(fifteen, fifteen, tg_recv).wait()
            top_mate = exchange(top_out.at[me.core], top_out.at[me.core], core_send, core_recv, mate)
            top_mate.start()

    home = lambda q, zh: (zh, me.bits["xb"], me.bits["xa"], q, me.bits["ya"], me.bits["yb"])
    for q in range(4):
        for zh in range(4):
            tile = acc[home(q, zh)]
            for zl in range(2):
                zsend[zh * 2 + zl, q] = tile[:, zl * 128 : zl * 128 + 128].astype(WIRE)
        tile = acc[home(q, me.zh)]
        for zl in range(2):
            zown[zl, q] = tile[:, zl * 128 : zl * 128 + 128]
    plane = [
        exchange(zsend.at[(me.z + j) % 8], zrecv.at[me.z], z_send.at[j - 1], z_recv,
                 me.at(z=(me.z + j) % 8))
        for j in range(1, 8)
    ]
    for copy in plane:
        copy.start()
    pltpu.make_async_copy(zrecv.at[pl.ds(0, 7)], zrecv.at[pl.ds(0, 7)], z_recv).wait()
    slot = 8 * me.core + 4 * me.zl + 2 * me.bits["ya"] + me.bits["yb"]
    for q in range(4):
        total = zown[me.zl, q]
        for j in range(1, 8):
            total = total + zrecv[(me.z + j) % 8, q].astype(F32)
        rows_out[0, slot, q] = total.astype(rows_out.dtype)
    mine = rows_out.at[0, slot]
    row_copies = [
        exchange(mine, mine, row_send.at[j - 1], row_recv, (me.r, (me.c + j) % 16))
        for j in range(1, 16)
    ]
    col_copies = [
        exchange(mine, rows_out.at[1, slot], col_send.at[j], col_recv, ((me.r + j) % 16, me.r))
        for j in range(16)
    ]
    for j in range(1, 16):
        col_copies[j].start()
        row_copies[j - 1].start()

    @pl.when(me.r != me.c)
    def _():
        col_copies[0].start()

    @pl.when(me.r == me.c)
    def _():
        rows_out[1, slot] = rows_out[0, slot]

    top_mate.wait()
    fifteen = rows_out.at[0, pl.ds(0, 15)]
    pltpu.make_async_copy(fifteen, fifteen, row_recv).wait()

    @pl.when(me.r != me.c)
    def _():
        pltpu.make_async_copy(rows_out.at[1], rows_out.at[1], col_recv).wait()
        col_copies[0].wait_send()

    @pl.when(me.r == me.c)
    def _():
        pltpu.make_async_copy(fifteen, fifteen, col_recv).wait()

    for copies in (row_copies, col_copies[1:], plane, top_plane, top_gather, shares):
        for copy in copies:
            copy.wait_send()
    for step in range(4):
        for q in range(4):
            top_copy(step, q).wait_send()
            for zh in range(4):
                main_copy(step, zh, q).wait_send()


def gather_rows(features):
    twos = lambda n: (2,) * n
    wire = lambda n: pltpu.VMEM((4, 4) + twos(n) + (32, BLOCK), WIRE)
    exact = lambda n: pltpu.VMEM((4,) + twos(n) + (8, BLOCK), F32)
    dma = pltpu.SemaphoreType.DMA
    return pl.pallas_call(
        gather_kernel,
        out_shape=(
            jax.ShapeDtypeStruct((2, 16, 4, 32, 128), WIRE),
            jax.ShapeDtypeStruct((2, 16, 4, 8, BLOCK), F32),
        ),
        in_specs=[pl.BlockSpec(memory_space=pl.ANY)],
        out_specs=(pl.BlockSpec(memory_space=pltpu.VMEM),) * 2,
        scratch_shapes=[
            pltpu.VMEM((TOKENS, HALF), jnp.bfloat16),
            pltpu.VMEM((TOKENS, HALF), jnp.bfloat16),
            pltpu.VMEM((TOKENS, PANEL), jnp.bfloat16),
            pltpu.VMEM((TOKENS, PANEL), jnp.bfloat16),
            pltpu.VMEM((PANEL, 2 * TOKENS), jnp.bfloat16),
            pltpu.VMEM((4, 2, 2, 4, 2, 2, 32, BLOCK), F32),
            pltpu.VMEM((4, 2, 2, 2, 2, 8, BLOCK), F32),
            *[wire(n) for n in (3, 2, 1, 0)],
            *[wire(n) for n in (3, 2, 1, 0)],
            *[exact(n) for n in (3, 2, 1, 0)],
            *[exact(n) for n in (3, 2, 1, 0)],
            pltpu.VMEM((8, 4, 32, 128), WIRE),
            pltpu.VMEM((8, 4, 32, 128), WIRE),
            pltpu.VMEM((2, 4, 32, 128), F32),
            pltpu.VMEM((8, 4, 8, BLOCK), F32),
            dma((5,)), dma((5,)), dma((5,)),
            dma((4, 4, 4)), dma((4, 4, 4)), dma((4, 4)), dma((4, 4)),
            dma((7,)), dma, dma((7,)), dma, dma((15,)), dma, dma, dma,
            dma((15,)), dma, dma((16,)), dma,
        ],
        compiler_params=pltpu.CompilerParams(
            collective_id=1, has_side_effects=True, vmem_limit_bytes=56 * 2**20
        ),
        cost_estimate=pl.CostEstimate(
            flops=2 * PANEL * 1024 * HALF, bytes_accessed=10 * 2**20, transcendentals=0
        ),
        name="reduce_gram",
    )(features)


def lane(tile, k):
    return jnp.broadcast_to(tile[:, k : k + 1], (8, 128))


def sublane(tile, k):
    return jnp.broadcast_to(tile[k : k + 1, :], (8, 128))


def pair_sum(terms):
    while len(terms) > 1:
        terms = [terms[2 * i] + terms[2 * i + 1] for i in range(len(terms) // 2)]
    return terms[0]


def inverse_128(tile):
    s = [tile[8 * i : 8 * i + 8] for i in range(16)]
    rows = lax.broadcasted_iota(jnp.int32, (8, 128), 0)
    cols = lax.broadcasted_iota(jnp.int32, (8, 128), 1)
    v = [jnp.where(cols == rows + 8 * i, 1.0, 0.0).astype(F32) for i in range(16)]
    out = []

    def collect(parts):
        whole = parts[7]
        for k in range(6, -1, -1):
            whole = jnp.where(rows == k, parts[k], whole)
        return whole

    for p in range(16):
        near = list(range(p, min(16, p + 2)))
        m = [[lane(s[g], 8 * p + k) for k in range(8)] for g in near]
        us, vs = [], []
        for k in range(8):
            inv = lax.rsqrt(sublane(m[0][k], k))
            u, w = sublane(s[p], k) * inv, sublane(v[p], k) * inv
            us.append(u)
            vs.append(w)
            scaled = [sublane(m[0][i], k) * inv for i in range(k + 1, 8)]
            for n, g in enumerate(near):
                if n == 0 and k == 7:
                    continue
                factor = m[n][k] * inv
                for i in range(k + 1, 8):
                    m[n][i] = m[n][i] - factor * scaled[i - k - 1]
                s[g] = s[g] - factor * u
                v[g] = v[g] - factor * w
        out.append(collect(vs))
        if p + 2 < 16:
            turned = collect(us).T
            for i in range(p + 2, 16):
                group = turned[8 * i : 8 * i + 8]
                factors = [lane(group, k) for k in range(8)]
                s[i] = s[i] - pair_sum([f * u for f, u in zip(factors, us)])
                v[i] = v[i] - pair_sum([f * w for f, w in zip(factors, vs)])
    return jnp.concatenate(out, 0)


def dot(left, right):
    return jnp.dot(left, right, precision=lax.Precision.HIGHEST, preferred_element_type=F32)


def dot_t(left, right):
    return lax.dot_general(
        left, right, (((1,), (1,)), ((), ())),
        precision=lax.Precision.HIGHEST, preferred_element_type=F32,
    )


def inverse_256(ref, start, out):
    lo, hi = pl.ds(start, 128), pl.ds(start + 128, 128)
    v1 = inverse_128(ref[lo, lo])
    below = dot_t(ref[hi, lo], v1)
    v2 = inverse_128(ref[hi, hi] - dot_t(below, below))
    out[:128, :128] = v1
    out[:128, 128:] = jnp.zeros((128, 128), F32)
    out[128:, :128] = -dot(v2, dot(below, v1))
    out[128:, 128:] = v2


def panel_kernel(rows, top, prior, panel_out, update_out, a, g, inv1, inv2, other):
    r, c = lax.axis_index("row"), lax.axis_index("col")
    for h in range(2):
        for q in range(4):
            for s in range(16):
                a[pl.ds(128 * q + 8 * s, 8), pl.ds(BLOCK * h, BLOCK)] = top[h, s, q]
    for b in range(4):
        at = pl.ds(128 * b, 128)
        i = lax.broadcasted_iota(jnp.int32, (128, 128), 0)
        j = lax.broadcasted_iota(jnp.int32, (128, 128), 1)
        a[at, at] = a[at, at] + jnp.where(i == j, prior[:, at], 0.0)
    for side in range(2):
        for h in range(2):
            for zl in range(2):
                for s in range(4):
                    for q in range(4):
                        g[side, pl.ds(128 * q + 32 * s, 32), pl.ds(BLOCK * h + 128 * zl, 128)] = rows[
                            side, 8 * h + 4 * zl + s, q
                        ].astype(F32)
        own = (r, c)[side]
        for b in range(2):

            @pl.when(own == b)
            def _():
                g[side, :, :BLOCK] = a[:, pl.ds(BLOCK * b, BLOCK)]

    inverse_256(a, 0, inv1)
    lead = dot_t(a[BLOCK:, :BLOCK], inv1[...])
    a[BLOCK:, BLOCK:] = a[BLOCK:, BLOCK:] - dot_t(lead, lead)
    inverse_256(a, BLOCK, inv2)

    for b in range(2):
        at = pl.ds(BLOCK * b, BLOCK)
        first = dot_t(g[0, :BLOCK, at].T, inv1[...])
        second = dot_t(g[0, BLOCK:, at].T - dot_t(first, lead), inv2[...])
        if b == 0:
            second = jnp.where(r == 0, 0.0, second)
        panel_out[0, at, :BLOCK] = first
        panel_out[0, at, BLOCK:] = second
    first = dot(inv1[...], g[1, :BLOCK])
    second = dot(inv2[...], g[1, BLOCK:] - dot(lead, first))
    other[:BLOCK] = first.astype(jnp.bfloat16)
    other[BLOCK:, :BLOCK] = jnp.where(c == 0, 0.0, second[:, :BLOCK]).astype(jnp.bfloat16)
    other[BLOCK:, BLOCK:] = second[:, BLOCK:].astype(jnp.bfloat16)
    update_out[0] = jnp.dot(
        panel_out[0].astype(jnp.bfloat16), other[...], preferred_element_type=F32
    ) * (1.0 / PANEL)


def on_device(features, prior):
    rows, top = gather_rows(features)
    panel, update = pl.pallas_call(
        panel_kernel,
        out_shape=(
            jax.ShapeDtypeStruct((1, PANEL, PANEL), F32),
            jax.ShapeDtypeStruct((1, PANEL, PANEL), F32),
        ),
        in_specs=[pl.BlockSpec(memory_space=pltpu.VMEM)] * 3,
        out_specs=(pl.BlockSpec(memory_space=pltpu.VMEM),) * 2,
        scratch_shapes=[
            pltpu.VMEM((PANEL, PANEL), F32),
            pltpu.VMEM((2, PANEL, PANEL), F32),
            pltpu.VMEM((BLOCK, BLOCK), F32),
            pltpu.VMEM((BLOCK, BLOCK), F32),
            pltpu.VMEM((PANEL, PANEL), jnp.bfloat16),
        ],
        compiler_params=pltpu.CompilerParams(vmem_limit_bytes=40 * 2**20),
        name="panels",
    )(rows, top, prior[None])
    return (panel, update[:, :, None, :])


def solution(mesh):
    placed = (P(("row", "col"), None), P())
    return jax.shard_map(
        on_device,
        mesh=mesh,
        in_specs=placed,
        out_specs=(P("row", None, None), P("row", None, "col", None)),
        check_vma=False,
    )
```

```python
import jax
import jax.numpy as jnp
from jax import lax
from jax.experimental import pallas as pl
from jax.experimental.pallas import tpu as pltpu
from jax.sharding import PartitionSpec as P

W = 8192
BLOCK = 256
PANEL = 512
TOKENS = 512
HALF = W // 2
MESH = pl.DeviceIdType.MESH
WIRE = jnp.bfloat16
F32 = jnp.float32
ORDERS = (
    ("xa", "xb", "ya", "yb"),
    ("xb", "ya", "yb", "xa"),
    ("ya", "yb", "xa", "xb"),
    ("yb", "xa", "xb", "ya"),
)
FULL = slice(None)


class Place:
    def __init__(self):
        self.r = lax.axis_index("row")
        self.c = lax.axis_index("col")
        self.x = self.r % 4
        self.y = (self.c // 2) % 4
        self.zh = self.r // 4
        self.zl = self.c // 8
        self.z = self.zh * 2 + self.zl
        self.core = self.c % 2
        self.bits = {
            "xa": ((self.x + 1) // 2) % 2,
            "xb": self.x // 2,
            "ya": ((self.y + 1) // 2) % 2,
            "yb": self.y // 2,
        }

    def at(self, x=None, y=None, z=None, core=None):
        x = self.x if x is None else x
        y = self.y if y is None else y
        z = self.z if z is None else z
        core = self.core if core is None else core
        return (z // 2 * 4 + x, z % 2 * 8 + y * 2 + core)

    def partner(self, dim):
        if dim == "xa":
            return self.at(x=self.x + 1 - 2 * (self.x % 2))
        if dim == "xb":
            return self.at(x=3 - self.x)
        if dim == "ya":
            return self.at(y=self.y + 1 - 2 * (self.y % 2))
        return self.at(y=3 - self.y)


def tile_index(place, quarter, zh, step, last):
    fixed = {}
    for k, dim in enumerate(ORDERS[quarter][: step + 1]):
        mine = place.bits[dim]
        fixed[dim] = mine if (k < step or last) else 1 - mine
    pick = lambda dim: fixed.get(dim, FULL)
    return (zh, pick("xb"), pick("xa"), quarter, pick("ya"), pick("yb"))


def top_index(place, quarter, step, last):
    _, xb, xa, _, ya, yb = tile_index(place, quarter, 0, step, last)
    return (quarter, ya, yb, xb, xa)


def panel_kernel(feat, prior, panel_out, other, rows_out, top_out, a, g, work, v, below, inv, lead, rest, own, theirs, lead_own, lead_their, lead_t, acc, top,
                  s0, s1, s2, s3, r0, r1, r2, r3, ts0, ts1, ts2, ts3, tr0, tr1, tr2, tr3,
                  zsend, zrecv, zown, topz,
                  load_sem, feat_send, feat_recv, step_send, step_recv, top_send, top_recv,
                  z_send, z_recv, tz_send, tz_recv, tg_send, tg_recv, core_send, core_recv,
                  row_send, row_recv, col_send, col_recv):
    me = Place()
    sends, recvs = (s0, s1, s2, s3), (r0, r1, r2, r3)
    tsends, trecvs = (ts0, ts1, ts2, ts3), (tr0, tr1, tr2, tr3)
    mate = me.at(core=1 - me.core)
    loads = [pltpu.make_async_copy(feat.at[:, pl.ds(0, PANEL)], lead_own, load_sem.at[0])]
    for i in range(4):
        loads.append(
            pltpu.make_async_copy(
                feat.at[:, pl.ds(pl.multiple_of(me.core * HALF + i * 1024, 1024), 1024)],
                own.at[:, pl.ds(i * 1024, 1024)],
                load_sem.at[i + 1],
            )
        )
    for load in loads:
        load.start()

    barrier = pltpu.get_barrier_semaphore()

    def greet(device):
        pl.semaphore_signal(barrier, inc=1, device_id=device, device_id_type=MESH)

    greet(mate)
    for dim in ORDERS[0]:
        greet(me.partner(dim))
    for j in range(1, 8):
        greet(me.at(z=(me.z + j) % 8))
    pl.semaphore_wait(barrier, 12)

    shares = [
        pltpu.make_async_remote_copy(
            src_ref=feat.at[:, pl.ds(0, PANEL)], dst_ref=lead_their,
            send_sem=feat_send.at[0], recv_sem=feat_recv.at[0],
            device_id=mate, device_id_type=MESH,
        )
    ]
    for i in range(4):
        shares.append(
            pltpu.make_async_remote_copy(
                src_ref=feat.at[:, pl.ds(pl.multiple_of((1 - me.core) * HALF + i * 1024, 1024), 1024)],
                dst_ref=theirs.at[:, pl.ds(i * 1024, 1024)],
                send_sem=feat_send.at[i + 1], recv_sem=feat_recv.at[i + 1],
                device_id=mate, device_id_type=MESH,
            )
        )
    for share in shares:
        share.start()

    loads[0].wait()
    lead_t[:, :TOKENS] = lead_own[...].T
    shares[0].wait_recv()
    lead_t[:, TOKENS:] = lead_their[...].T

    def products(left, right):
        return jnp.dot(lead_t[:, :TOKENS], left, preferred_element_type=F32) + jnp.dot(
            lead_t[:, TOKENS:], right, preferred_element_type=F32
        )

    lanes = pl.ds(pl.multiple_of(me.core * BLOCK, BLOCK), BLOCK)
    top[...] = products(lead_own[:, lanes], lead_their[:, lanes]).reshape(4, 2, 2, 2, 2, 8, BLOCK)

    def exchange(src, dst, send, recv, device):
        return pltpu.make_async_remote_copy(
            src_ref=src, dst_ref=dst, send_sem=send, recv_sem=recv,
            device_id=device, device_id_type=MESH,
        )

    def top_copy(step, q):
        return exchange(
            tsends[step].at[q], trecvs[step].at[q], top_send.at[step, q], top_recv.at[step, q],
            me.partner(ORDERS[q][step]),
        )

    def top_start(step):
        for q in range(4):
            tsends[step][q] = top[top_index(me, q, step, False)]
            top_copy(step, q).start()

    def top_finish(step):
        for q in range(4):
            top_copy(step, q).wait_recv()
            at = top_index(me, q, step, True)
            top[at] = top[at] + trecvs[step][q]

    def main_copy(step, zh, q):
        return exchange(
            sends[step].at[zh, q], recvs[step].at[zh, q],
            step_send.at[step, zh, q], step_recv.at[step, zh, q],
            me.partner(ORDERS[q][step]),
        )

    def main_start(step, zh):
        for q in range(4):
            sends[step][zh, q] = acc[tile_index(me, q, zh, step, False)].astype(WIRE)
            main_copy(step, zh, q).start()

    def main_finish(step, zh):
        for q in range(4):
            main_copy(step, zh, q).wait_recv()
            at = tile_index(me, q, zh, step, True)
            acc[at] = acc[at] + recvs[step][zh, q].astype(F32)

    def multiply(zh):
        loads[zh + 1].wait()
        shares[zh + 1].wait_recv()

        def body(p, carry):
            xb, xa = p // 2, p % 2
            x = 2 * xb + (xb + xa) % 2
            at = pl.ds(pl.multiple_of((zh * 4 + x) * BLOCK, BLOCK), BLOCK)
            acc[zh, xb, xa] = products(own[:, at], theirs[:, at]).reshape(4, 2, 2, 32, BLOCK)
            return carry

        lax.fori_loop(0, 4, body, 0)

    my_top = (me.bits["ya"], me.bits["yb"], me.bits["xb"], me.bits["xa"])
    my_slot = 8 * my_top[0] + 4 * my_top[1] + 2 * my_top[2] + my_top[3]
    top_start(0)
    for wave in range(8):
        if wave >= 1 and wave <= 4:
            top_finish(wave - 1)
            if wave < 4:
                top_start(wave)
            else:
                for q in range(4):
                    topz[me.z, q] = top[(q,) + my_top]
                top_plane = [
                    exchange(topz.at[me.z], topz.at[me.z], tz_send.at[j - 1], tz_recv,
                             me.at(z=(me.z + j) % 8))
                    for j in range(1, 8)
                ]
                for copy in top_plane:
                    copy.start()
        if wave < 4:
            multiply(wave)
            main_start(0, wave)
        if wave == 5:
            pltpu.make_async_copy(topz.at[pl.ds(0, 7)], topz.at[pl.ds(0, 7)], tz_recv).wait()
            for q in range(4):
                total = topz[0, q]
                for z in range(1, 8):
                    total = total + topz[z, q]
                top_out[me.core, my_slot, q] = total
            top_gather = [
                exchange(top_out.at[me.core, my_slot], top_out.at[me.core, my_slot],
                         tg_send.at[j - 1], tg_recv,
                         me.at(x=(me.x + j) % 4, y=(me.y + j // 4) % 4))
                for j in range(1, 16)
            ]
            for copy in top_gather:
                copy.start()
        for step in range(4):
            zh = wave - step - 1
            if 0 <= zh < 4:
                main_finish(step, zh)
                if step < 3:
                    main_start(step + 1, zh)
        if wave == 6:
            fifteen = top_out.at[me.core, pl.ds(0, 15)]
            pltpu.make_async_copy(fifteen, fifteen, tg_recv).wait()
            top_mate = exchange(top_out.at[me.core], top_out.at[me.core], core_send, core_recv, mate)
            top_mate.start()

    home = lambda q, zh: (zh, me.bits["xb"], me.bits["xa"], q, me.bits["ya"], me.bits["yb"])
    for q in range(4):
        for zh in range(4):
            tile = acc[home(q, zh)]
            for zl in range(2):
                zsend[zh * 2 + zl, q] = tile[:, zl * 128 : zl * 128 + 128].astype(WIRE)
        tile = acc[home(q, me.zh)]
        for zl in range(2):
            zown[zl, q] = tile[:, zl * 128 : zl * 128 + 128]
    plane = [
        exchange(zsend.at[(me.z + j) % 8], zrecv.at[me.z], z_send.at[j - 1], z_recv,
                 me.at(z=(me.z + j) % 8))
        for j in range(1, 8)
    ]
    for copy in plane:
        copy.start()
    top_mate.wait()
    for h in range(2):
        for q in range(4):
            for t in range(16):
                a[pl.ds(128 * q + 8 * t, 8), pl.ds(BLOCK * h, BLOCK)] = top_out[h, t, q]
    for b in range(4):
        at = pl.ds(128 * b, 128)
        i = lax.broadcasted_iota(jnp.int32, (128, 128), 0)
        j = lax.broadcasted_iota(jnp.int32, (128, 128), 1)
        a[at, at] = a[at, at] + jnp.where(i == j, prior[:, at], 0.0)

    slot = 8 * me.core + 4 * me.zl + 2 * me.bits["ya"] + me.bits["yb"]
    mine = rows_out.at[0, slot]
    row_copies = [
        exchange(mine, mine, row_send.at[j - 1], row_recv, (me.r, (me.c + j) % 16))
        for j in range(1, 16)
    ]
    col_copies = [
        exchange(mine, rows_out.at[1, slot], col_send.at[j], col_recv, ((me.r + j) % 16, me.r))
        for j in range(16)
    ]

    def finish_z():
        pltpu.make_async_copy(zrecv.at[pl.ds(0, 7)], zrecv.at[pl.ds(0, 7)], z_recv).wait()
        for q in range(4):
            total = zown[me.zl, q]
            for j in range(1, 8):
                total = total + zrecv[(me.z + j) % 8, q].astype(F32)
            rows_out[0, slot, q] = total.astype(rows_out.dtype)
        for j in range(1, 16):
            col_copies[j].start()
            row_copies[j - 1].start()

        @pl.when(me.r != me.c)
        def _():
            col_copies[0].start()

        @pl.when(me.r == me.c)
        def _():
            rows_out[1, slot] = rows_out[0, slot]

    def second_tile(tile):
        below[...] = dot_t(tile[128:BLOCK, :128], v[0])
        work[...] = tile[128:BLOCK, 128:BLOCK] - dot_t(below[...], below[...])

    def finish_inverse(half):
        inv[half, :128, :128] = v[0]
        inv[half, :128, 128:] = jnp.zeros((128, 128), F32)
        inv[half, 128:, :128] = -dot(v[1], dot(below[...], v[0]))
        inv[half, 128:, 128:] = v[1]

    def factorise(b, carry):
        @pl.when(b == 0)
        def _():
            work[...] = a[:128, :128]

        @pl.when(b == 1)
        def _():
            finish_z()
            second_tile(a)

        @pl.when(b == 2)
        def _():
            finish_inverse(0)
            lead[...] = dot_t(a[BLOCK:, :BLOCK], inv[0])
            rest[...] = a[BLOCK:, BLOCK:] - dot_t(lead[...], lead[...])
            work[...] = rest[:128, :128]

        @pl.when(b == 3)
        def _():
            second_tile(rest)

        v[b % 2] = inverse_128(work[...])
        return carry

    lax.fori_loop(0, 4, factorise, 0)
    finish_inverse(1)

    fifteen = rows_out.at[0, pl.ds(0, 15)]
    pltpu.make_async_copy(fifteen, fifteen, row_recv).wait()

    @pl.when(me.r != me.c)
    def _():
        pltpu.make_async_copy(rows_out.at[1], rows_out.at[1], col_recv).wait()
        col_copies[0].wait_send()

    @pl.when(me.r == me.c)
    def _():
        pltpu.make_async_copy(fifteen, fifteen, col_recv).wait()

    for side in range(2):
        for h in range(2):
            for zl in range(2):
                for t in range(4):
                    for q in range(4):
                        g[side, pl.ds(128 * q + 32 * t, 32), pl.ds(BLOCK * h + 128 * zl, 128)] = (
                            rows_out[side, 8 * h + 4 * zl + t, q].astype(F32)
                        )
        for b in range(2):

            @pl.when((me.r, me.c)[side] == b)
            def _():
                g[side, :, :BLOCK] = a[:, pl.ds(BLOCK * b, BLOCK)]

    for b in range(2):
        at = pl.ds(BLOCK * b, BLOCK)
        first = dot_t(g[0, :BLOCK, at].T, inv[0])
        second = dot_t(g[0, BLOCK:, at].T - dot_t(first, lead[...]), inv[1])
        if b == 0:
            second = jnp.where(me.r == 0, 0.0, second)
        panel_out[at, :BLOCK] = first
        panel_out[at, BLOCK:] = second
    first = dot(inv[0], g[1, :BLOCK])
    second = dot(inv[1], g[1, BLOCK:] - dot(lead[...], first))
    other[:BLOCK] = first.astype(jnp.bfloat16)
    other[BLOCK:, :BLOCK] = jnp.where(me.c == 0, 0.0, second[:, :BLOCK]).astype(jnp.bfloat16)
    other[BLOCK:, BLOCK:] = second[:, BLOCK:].astype(jnp.bfloat16)

    for copies in (row_copies, col_copies[1:], plane, top_plane, top_gather, shares):
        for copy in copies:
            copy.wait_send()
    for step in range(4):
        for q in range(4):
            top_copy(step, q).wait_send()
            for zh in range(4):
                main_copy(step, zh, q).wait_send()


def panels(features, prior):
    twos = lambda n: (2,) * n
    wire = lambda n: pltpu.VMEM((4, 4) + twos(n) + (32, BLOCK), WIRE)
    exact = lambda n: pltpu.VMEM((4,) + twos(n) + (8, BLOCK), F32)
    dma = pltpu.SemaphoreType.DMA
    return pl.pallas_call(
        panel_kernel,
        out_shape=(
            jax.ShapeDtypeStruct((PANEL, PANEL), F32),
            jax.ShapeDtypeStruct((PANEL, PANEL), jnp.bfloat16),
        ),
        in_specs=[pl.BlockSpec(memory_space=pl.ANY), pl.BlockSpec(memory_space=pltpu.VMEM)],
        out_specs=(pl.BlockSpec(memory_space=pltpu.VMEM),) * 2,
        scratch_shapes=[
            pltpu.VMEM((2, 16, 4, 32, 128), WIRE),
            pltpu.VMEM((2, 16, 4, 8, BLOCK), F32),
            pltpu.VMEM((PANEL, PANEL), F32),
            pltpu.VMEM((2, PANEL, PANEL), F32),
            pltpu.VMEM((128, 128), F32),
            pltpu.VMEM((2, 128, 128), F32),
            pltpu.VMEM((128, 128), F32),
            pltpu.VMEM((2, BLOCK, BLOCK), F32),
            pltpu.VMEM((BLOCK, BLOCK), F32),
            pltpu.VMEM((BLOCK, BLOCK), F32),
            pltpu.VMEM((TOKENS, HALF), jnp.bfloat16),
            pltpu.VMEM((TOKENS, HALF), jnp.bfloat16),
            pltpu.VMEM((TOKENS, PANEL), jnp.bfloat16),
            pltpu.VMEM((TOKENS, PANEL), jnp.bfloat16),
            pltpu.VMEM((PANEL, 2 * TOKENS), jnp.bfloat16),
            pltpu.VMEM((4, 2, 2, 4, 2, 2, 32, BLOCK), F32),
            pltpu.VMEM((4, 2, 2, 2, 2, 8, BLOCK), F32),
            *[wire(n) for n in (3, 2, 1, 0)],
            *[wire(n) for n in (3, 2, 1, 0)],
            *[exact(n) for n in (3, 2, 1, 0)],
            *[exact(n) for n in (3, 2, 1, 0)],
            pltpu.VMEM((8, 4, 32, 128), WIRE),
            pltpu.VMEM((8, 4, 32, 128), WIRE),
            pltpu.VMEM((2, 4, 32, 128), F32),
            pltpu.VMEM((8, 4, 8, BLOCK), F32),
            dma((5,)), dma((5,)), dma((5,)),
            dma((4, 4, 4)), dma((4, 4, 4)), dma((4, 4)), dma((4, 4)),
            dma((7,)), dma, dma((7,)), dma, dma((15,)), dma, dma, dma,
            dma((15,)), dma, dma((16,)), dma,
        ],
        compiler_params=pltpu.CompilerParams(
            collective_id=1, has_side_effects=True, vmem_limit_bytes=56 * 2**20
        ),
        cost_estimate=pl.CostEstimate(
            flops=2 * PANEL * 1024 * HALF, bytes_accessed=10 * 2**20, transcendentals=0
        ),
        name="panels",
    )(features, prior)


def lane(tile, k):
    return jnp.broadcast_to(tile[:, k : k + 1], (8, 128))


def sublane(tile, k):
    return jnp.broadcast_to(tile[k : k + 1, :], (8, 128))


def pair_sum(terms):
    while len(terms) > 1:
        terms = [terms[2 * i] + terms[2 * i + 1] for i in range(len(terms) // 2)]
    return terms[0]


def inverse_128(tile):
    s = [tile[8 * i : 8 * i + 8] for i in range(16)]
    rows = lax.broadcasted_iota(jnp.int32, (8, 128), 0)
    cols = lax.broadcasted_iota(jnp.int32, (8, 128), 1)
    v = [jnp.where(cols == rows + 8 * i, 1.0, 0.0).astype(F32) for i in range(16)]
    out = []

    def collect(parts):
        whole = parts[7]
        for k in range(6, -1, -1):
            whole = jnp.where(rows == k, parts[k], whole)
        return whole

    for p in range(16):
        near = list(range(p, min(16, p + 2)))
        m = [[lane(s[g], 8 * p + k) for k in range(8)] for g in near]
        us, vs = [], []
        for k in range(8):
            inv = lax.rsqrt(sublane(m[0][k], k))
            u, w = sublane(s[p], k) * inv, sublane(v[p], k) * inv
            us.append(u)
            vs.append(w)
            scaled = [sublane(m[0][i], k) * inv for i in range(k + 1, 8)]
            for n, g in enumerate(near):
                if n == 0 and k == 7:
                    continue
                factor = m[n][k] * inv
                for i in range(k + 1, 8):
                    m[n][i] = m[n][i] - factor * scaled[i - k - 1]
                s[g] = s[g] - factor * u
                v[g] = v[g] - factor * w
        out.append(collect(vs))
        if p + 2 < 16:
            turned = collect(us).T
            for i in range(p + 2, 16):
                group = turned[8 * i : 8 * i + 8]
                factors = [lane(group, k) for k in range(8)]
                s[i] = s[i] - pair_sum([f * u for f, u in zip(factors, us)])
                v[i] = v[i] - pair_sum([f * w for f, w in zip(factors, vs)])
    return jnp.concatenate(out, 0)


def dot(left, right):
    return jnp.dot(left, right, precision=lax.Precision.HIGHEST, preferred_element_type=F32)


def dot_t(left, right):
    return lax.dot_general(
        left, right, (((1,), (1,)), ((), ())),
        precision=lax.Precision.HIGHEST, preferred_element_type=F32,
    )


def finish_kernel(panel, other, panel_out, update_out, product, sem):
    panel_copy = pltpu.make_async_copy(panel, panel_out.at[0], sem.at[0])
    panel_copy.start()
    product[...] = jnp.dot(
        panel[...].astype(jnp.bfloat16), other[...], preferred_element_type=F32
    ) * (1.0 / PANEL)
    product_copy = pltpu.make_async_copy(product, update_out.at[0, :, 0, :], sem.at[1])
    product_copy.start()
    panel_copy.wait()
    product_copy.wait()


def on_device(features, prior):
    panel, other = panels(features, prior[None])
    return pl.pallas_call(
        finish_kernel,
        out_shape=(
            jax.ShapeDtypeStruct((1, PANEL, PANEL), F32),
            jax.ShapeDtypeStruct((1, PANEL, 1, PANEL), F32),
        ),
        in_specs=[pl.BlockSpec(memory_space=pltpu.VMEM)] * 2,
        out_specs=(pl.BlockSpec(memory_space=pl.ANY),) * 2,
        scratch_shapes=[pltpu.VMEM((PANEL, PANEL), F32), pltpu.SemaphoreType.DMA((2,))],
        name="product",
    )(panel, other)


def solution(mesh):
    placed = (P(("row", "col"), None), P())
    return jax.shard_map(
        on_device,
        mesh=mesh,
        in_specs=placed,
        out_specs=(P("row", None, None), P("row", None, "col", None)),
        check_vma=False,
    )
```

```python
import jax
import jax.numpy as jnp
from jax import lax
from jax.experimental import pallas as pl
from jax.experimental.pallas import tpu as pltpu
from jax.sharding import PartitionSpec as P

W = 8192
BLOCK = 256
PANEL = 512
TOKENS = 512
HALF = W // 2
MESH = pl.DeviceIdType.MESH
WIRE = jnp.bfloat16
F32 = jnp.float32
ORDERS = (
    ("xa", "xb", "ya", "yb"),
    ("xb", "ya", "yb", "xa"),
    ("ya", "yb", "xa", "xb"),
    ("yb", "xa", "xb", "ya"),
)
FULL = slice(None)
TOP_WAVES = {3: 1, 5: 2}
LAST_WAVE, END_Z, PASS = (0, 4), (1, 0), (3, 12)


class Place:
    def __init__(self):
        self.r = lax.axis_index("row")
        self.c = lax.axis_index("col")
        self.x = self.r % 4
        self.y = (self.c // 2) % 4
        self.zh = self.r // 4
        self.zl = self.c // 8
        self.z = self.zh * 2 + self.zl
        self.core = self.c % 2
        self.bits = {
            "xa": ((self.x + 1) // 2) % 2,
            "xb": self.x // 2,
            "ya": ((self.y + 1) // 2) % 2,
            "yb": self.y // 2,
        }

    def at(self, x=None, y=None, z=None, core=None):
        x = self.x if x is None else x
        y = self.y if y is None else y
        z = self.z if z is None else z
        core = self.core if core is None else core
        return (z // 2 * 4 + x, z % 2 * 8 + y * 2 + core)

    def partner(self, dim):
        if dim == "xa":
            return self.at(x=self.x + 1 - 2 * (self.x % 2))
        if dim == "xb":
            return self.at(x=3 - self.x)
        if dim == "ya":
            return self.at(y=self.y + 1 - 2 * (self.y % 2))
        return self.at(y=3 - self.y)


def tile_index(place, quarter, zh, step, last):
    fixed = {}
    for k, dim in enumerate(ORDERS[quarter][: step + 1]):
        mine = place.bits[dim]
        fixed[dim] = mine if (k < step or last) else 1 - mine
    pick = lambda dim: fixed.get(dim, FULL)
    return (zh, pick("xb"), pick("xa"), quarter, pick("ya"), pick("yb"))


def strip(y):
    return 2 * (((y + 1) // 2) % 2) + y // 2


def top_slot(x, y):
    return 4 * strip(y) + 2 * (x // 2) + ((x + 1) // 2) % 2


def panel_kernel(feat, prior, panel_out, other, rows_out, top_out, a, g, work, v, below, inv, lead, rest, own, theirs, lead_own, lead_their, lead_t, acc, top, top_parts,
                  s0, s1, s2, s3, r0, r1, r2, r3,
                  zsend, zrecv, zown, topz,
                  load_sem, feat_send, feat_recv, step_send, step_recv, ts_send, ts_recv,
                  z_send, z_recv, tz_send, tz_recv, tg_send, tg_recv, core_send, core_recv,
                  row_send, row_recv, col_send, col_recv, pass_send, pass_recv):
    me = Place()
    sends, recvs = (s0, s1, s2, s3), (r0, r1, r2, r3)
    mate = me.at(core=1 - me.core)
    loads = [pltpu.make_async_copy(feat.at[:, pl.ds(0, PANEL)], lead_own, load_sem.at[0])]
    for i in range(4):
        loads.append(
            pltpu.make_async_copy(
                feat.at[:, pl.ds(pl.multiple_of(me.core * HALF + i * 1024, 1024), 1024)],
                own.at[:, pl.ds(i * 1024, 1024)],
                load_sem.at[i + 1],
            )
        )
    for load in loads:
        load.start()

    barrier = pltpu.get_barrier_semaphore()

    def greet(device):
        pl.semaphore_signal(barrier, inc=1, device_id=device, device_id_type=MESH)

    greet(mate)
    for j in range(1, 16):
        greet(me.at(x=(me.x + j) % 4, y=(me.y + j // 4) % 4))
    for j in range(1, 8):
        greet(me.at(z=(me.z + j) % 8))
    pl.semaphore_wait(barrier, 23)

    shares = [
        pltpu.make_async_remote_copy(
            src_ref=feat.at[:, pl.ds(0, PANEL)], dst_ref=lead_their,
            send_sem=feat_send.at[0], recv_sem=feat_recv.at[0],
            device_id=mate, device_id_type=MESH,
        )
    ]
    for i in range(4):
        shares.append(
            pltpu.make_async_remote_copy(
                src_ref=feat.at[:, pl.ds(pl.multiple_of((1 - me.core) * HALF + i * 1024, 1024), 1024)],
                dst_ref=theirs.at[:, pl.ds(i * 1024, 1024)],
                send_sem=feat_send.at[i + 1], recv_sem=feat_recv.at[i + 1],
                device_id=mate, device_id_type=MESH,
            )
        )
    for share in shares:
        share.start()

    loads[0].wait()
    lead_t[:, :TOKENS] = lead_own[...].T
    shares[0].wait_recv()
    lead_t[:, TOKENS:] = lead_their[...].T

    def products(left, right):
        return jnp.dot(lead_t[:, :TOKENS], left, preferred_element_type=F32) + jnp.dot(
            lead_t[:, TOKENS:], right, preferred_element_type=F32
        )

    lanes = pl.ds(pl.multiple_of(me.core * BLOCK, BLOCK), BLOCK)
    square = products(lead_own[:, lanes], lead_their[:, lanes]).reshape(4, 16, 8, BLOCK)
    for t in range(16):
        top[t] = square[:, t]

    def exchange(src, dst, send, recv, device):
        return pltpu.make_async_remote_copy(
            src_ref=src, dst_ref=dst, send_sem=send, recv_sem=recv,
            device_id=device, device_id_type=MESH,
        )

    def main_copy(step, zh, q):
        return exchange(
            sends[step].at[zh, q], recvs[step].at[zh, q],
            step_send.at[step, zh, q], step_recv.at[step, zh, q],
            me.partner(ORDERS[q][step]),
        )

    def main_start(step, zh):
        for q in range(4):
            sends[step][zh, q] = acc[tile_index(me, q, zh, step, False)].astype(WIRE)
            main_copy(step, zh, q).start()

    def main_finish(step, zh):
        for q in range(4):
            main_copy(step, zh, q).wait_recv()
            at = tile_index(me, q, zh, step, True)
            acc[at] = acc[at] + recvs[step][zh, q].astype(F32)

    def multiply(zh):
        loads[zh + 1].wait()
        shares[zh + 1].wait_recv()

        def body(p, carry):
            xb, xa = p // 2, p % 2
            x = 2 * xb + (xb + xa) % 2
            at = pl.ds(pl.multiple_of((zh * 4 + x) * BLOCK, BLOCK), BLOCK)
            acc[zh, xb, xa] = products(own[:, at], theirs[:, at]).reshape(4, 2, 2, 32, BLOCK)
            return carry

        lax.fori_loop(0, 4, body, 0)

    my_slot = top_slot(me.x, me.y)
    plane_at = [((me.x + j) % 4, (me.y + j // 4) % 4) for j in range(1, 16)]
    top_sums = [
        exchange(top.at[top_slot(x, y)], top_parts.at[my_slot], ts_send.at[j], ts_recv, me.at(x=x, y=y))
        for j, (x, y) in enumerate(plane_at)
    ]
    top_column = [
        exchange(topz.at[me.z], topz.at[me.z], tz_send.at[j - 1], tz_recv, me.at(z=(me.z + j) % 8))
        for j in range(1, 8)
    ]
    top_gather = [
        exchange(top_out.at[me.core, my_slot], top_out.at[me.core, my_slot],
                 tg_send.at[j], tg_recv.at[(j + 1) // 4], me.at(x=x, y=y))
        for j, (x, y) in enumerate(plane_at)
    ]
    top_pass = []
    for k in range(4):
        four = top_out.at[me.core, pl.ds(4 * strip((me.y + 4 - k) % 4), 4)]
        top_pass.append(exchange(four, four, core_send.at[k], core_recv.at[k], mate))

    def top_stage(stage):
        if stage == 0:
            for copy in top_sums:
                copy.start()
        if stage == 1:
            fifteen = top_parts.at[pl.ds(0, 15)]
            pltpu.make_async_copy(fifteen, fifteen, ts_recv).wait()
            top_parts[my_slot] = top[my_slot]
            topz[me.z] = pair_sum([top_parts[t] for t in range(16)])
            for copy in top_column:
                copy.start()
        if stage == 2:
            seven = topz.at[pl.ds(0, 7)]
            pltpu.make_async_copy(seven, seven, tz_recv).wait()
            top_out[me.core, my_slot] = pair_sum([topz[z] for z in range(8)])
            for copy in top_gather:
                copy.start()
        if stage == 3:
            for k in range(4):
                some = top_out.at[me.core, pl.ds(0, 4 if k else 3)]
                pltpu.make_async_copy(some, some, tg_recv.at[k]).wait()
                top_pass[k].start()

    home = lambda q, zh: (zh, me.bits["xb"], me.bits["xa"], q, me.bits["ya"], me.bits["yb"])
    column = [exchange(zsend.at[z], zrecv.at[me.z], z_send.at[z], z_recv, me.at(z=z)) for z in range(8)]

    def send_strips(zh):
        for q in range(4):
            tile = acc[home(q, zh)]
            for zl in range(2):
                zsend[zh * 2 + zl, q] = tile[:, zl * 128 : zl * 128 + 128].astype(WIRE)
        for z in (2 * zh, 2 * zh + 1):
            pl.when(me.z != z)(column[z].start)

    def wave(number):
        if number < 4:
            multiply(number)
            main_start(0, number)
        for step in range(4):
            zh = number - step - 1
            if 0 <= zh < 4:
                main_finish(step, zh)
                if step < 3:
                    main_start(step + 1, zh)
                else:
                    send_strips(zh)

    top_stage(0)
    for number in range(7):
        if number in TOP_WAVES:
            top_stage(TOP_WAVES[number])
        wave(number)
    top_stage(3)

    for copy in top_pass:
        copy.wait_recv()
    for h in range(2):
        for q in range(4):
            for t in range(16):
                a[pl.ds(128 * q + 8 * t, 8), pl.ds(BLOCK * h, BLOCK)] = top_out[h, t, q]
    for b in range(4):
        at = pl.ds(128 * b, 128)
        i = lax.broadcasted_iota(jnp.int32, (128, 128), 0)
        j = lax.broadcasted_iota(jnp.int32, (128, 128), 1)
        a[at, at] = a[at, at] + jnp.where(i == j, prior[at].reshape(1, 128), 0.0)

    slot = 8 * me.core + 4 * me.zl + 2 * me.bits["ya"] + me.bits["yb"]
    mine = rows_out.at[0, slot]
    row_copies = [
        exchange(mine, mine, row_send.at[j - 1], row_recv,
                 me.at(y=(me.y + j) % 4, z=2 * me.zh + (me.zl + j // 4) % 2))
        for j in range(1, 8)
    ]
    eight = rows_out.at[0, pl.ds(8 * me.core, 8)]
    row_pass = exchange(eight, eight, pass_send, pass_recv, mate)
    col_copies = [
        exchange(mine, rows_out.at[1, slot], col_send.at[j], col_recv, ((me.r + j) % 16, me.r))
        for j in range(16)
    ]

    def last_wave():
        wave(7)

    def finish_z():
        for q in range(4):
            tile = acc[home(q, me.zh)]
            for zl in range(2):
                zown[zl, q] = tile[:, zl * 128 : zl * 128 + 128]
        pltpu.make_async_copy(zrecv.at[pl.ds(0, 7)], zrecv.at[pl.ds(0, 7)], z_recv).wait()
        for q in range(4):
            total = zown[me.zl, q]
            for j in range(1, 8):
                total = total + zrecv[(me.z + j) % 8, q].astype(F32)
            rows_out[0, slot, q] = total.astype(rows_out.dtype)
        for copy in row_copies + col_copies[1:]:
            copy.start()

        @pl.when(me.r != me.c)
        def _():
            col_copies[0].start()

        @pl.when(me.r == me.c)
        def _():
            rows_out[1, slot] = rows_out[0, slot]

    def second_tile(tile):
        below[...] = dot_t(tile[128:BLOCK, :128], v[0])
        work[...] = tile[128:BLOCK, 128:BLOCK] - dot_t(below[...], below[...])

    def finish_inverse(half):
        inv[half, :128, :128] = v[0]
        inv[half, :128, 128:] = jnp.zeros((128, 128), F32)
        inv[half, 128:, :128] = -dot(v[1], dot(below[...], v[0]))
        inv[half, 128:, 128:] = v[1]

    def pass_rows():
        seven = rows_out.at[0, pl.ds(0, 7)]
        pltpu.make_async_copy(seven, seven, row_recv).wait()
        row_pass.start()

    def factorise(b, carry):
        @pl.when(b == 0)
        def _():
            work[...] = a[:128, :128]

        @pl.when(b == 1)
        def _():
            second_tile(a)

        @pl.when(b == 2)
        def _():
            finish_inverse(0)
            lead[...] = dot_t(a[BLOCK:, :BLOCK], inv[0])
            rest[...] = a[BLOCK:, BLOCK:] - dot_t(lead[...], lead[...])
            work[...] = rest[:128, :128]

        @pl.when(b == 3)
        def _():
            second_tile(rest)

        def between(panel):
            for when, act in ((LAST_WAVE, last_wave), (END_Z, finish_z), (PASS, pass_rows)):
                if panel == when[1]:
                    pl.when(b == when[0])(act)

        v[b % 2] = inverse_128(work[...], between)
        return carry

    lax.fori_loop(0, 4, factorise, 0)
    finish_inverse(1)

    def assemble(side):
        for h in range(2):
            for zl in range(2):
                for t in range(4):
                    for q in range(4):
                        g[side, pl.ds(128 * q + 32 * t, 32), pl.ds(BLOCK * h + 128 * zl, 128)] = (
                            rows_out[side, 8 * h + 4 * zl + t, q].astype(F32)
                        )
        for b in range(2):

            @pl.when((me.r, me.c)[side] == b)
            def _():
                g[side, :, :BLOCK] = a[:, pl.ds(BLOCK * b, BLOCK)]

    row_pass.wait_recv()
    assemble(0)
    for b in range(2):
        at = pl.ds(BLOCK * b, BLOCK)
        first = dot_t(g[0, :BLOCK, at].T, inv[0])
        second = dot_t(g[0, BLOCK:, at].T - dot_t(first, lead[...]), inv[1])
        if b == 0:
            second = jnp.where(me.r == 0, 0.0, second)
        panel_out[at, :BLOCK] = first
        panel_out[at, BLOCK:] = second

    @pl.when(me.r != me.c)
    def _():
        pltpu.make_async_copy(rows_out.at[1], rows_out.at[1], col_recv).wait()
        col_copies[0].wait_send()

    @pl.when(me.r == me.c)
    def _():
        fifteen = rows_out.at[1, pl.ds(0, 15)]
        pltpu.make_async_copy(fifteen, fifteen, col_recv).wait()

    assemble(1)
    first = dot(inv[0], g[1, :BLOCK])
    second = dot(inv[1], g[1, BLOCK:] - dot(lead[...], first))
    other[:BLOCK] = first.astype(jnp.bfloat16)
    other[BLOCK:, :BLOCK] = jnp.where(me.c == 0, 0.0, second[:, :BLOCK]).astype(jnp.bfloat16)
    other[BLOCK:, BLOCK:] = second[:, BLOCK:].astype(jnp.bfloat16)

    for copies in (row_copies, col_copies[1:], shares, [row_pass]):
        for copy in copies:
            copy.wait_send()
    for z in range(8):
        pl.when(me.z != z)(column[z].wait_send)
    for copies in (top_sums, top_column, top_gather, top_pass):
        for copy in copies:
            copy.wait_send()
    for step in range(4):
        for q in range(4):
            for zh in range(4):
                main_copy(step, zh, q).wait_send()


def panels(features, prior):
    twos = lambda n: (2,) * n
    wire = lambda n: pltpu.VMEM((4, 4) + twos(n) + (32, BLOCK), WIRE)
    dma = pltpu.SemaphoreType.DMA
    return pl.pallas_call(
        panel_kernel,
        out_shape=(
            jax.ShapeDtypeStruct((PANEL, PANEL), F32),
            jax.ShapeDtypeStruct((PANEL, PANEL), jnp.bfloat16),
        ),
        in_specs=[pl.BlockSpec(memory_space=pl.ANY), pl.BlockSpec(memory_space=pltpu.VMEM)],
        out_specs=(pl.BlockSpec(memory_space=pltpu.VMEM),) * 2,
        scratch_shapes=[
            pltpu.VMEM((2, 16, 4, 32, 128), WIRE),
            pltpu.VMEM((2, 16, 4, 8, BLOCK), F32),
            pltpu.VMEM((PANEL, PANEL), F32),
            pltpu.VMEM((2, PANEL, PANEL), F32),
            pltpu.VMEM((128, 128), F32),
            pltpu.VMEM((2, 128, 128), F32),
            pltpu.VMEM((128, 128), F32),
            pltpu.VMEM((2, BLOCK, BLOCK), F32),
            pltpu.VMEM((BLOCK, BLOCK), F32),
            pltpu.VMEM((BLOCK, BLOCK), F32),
            pltpu.VMEM((TOKENS, HALF), jnp.bfloat16),
            pltpu.VMEM((TOKENS, HALF), jnp.bfloat16),
            pltpu.VMEM((TOKENS, PANEL), jnp.bfloat16),
            pltpu.VMEM((TOKENS, PANEL), jnp.bfloat16),
            pltpu.VMEM((PANEL, 2 * TOKENS), jnp.bfloat16),
            pltpu.VMEM((4, 2, 2, 4, 2, 2, 32, BLOCK), F32),
            pltpu.VMEM((16, 4, 8, BLOCK), F32),
            pltpu.VMEM((16, 4, 8, BLOCK), F32),
            *[wire(n) for n in (3, 2, 1, 0)],
            *[wire(n) for n in (3, 2, 1, 0)],
            pltpu.VMEM((8, 4, 32, 128), WIRE),
            pltpu.VMEM((8, 4, 32, 128), WIRE),
            pltpu.VMEM((2, 4, 32, 128), F32),
            pltpu.VMEM((8, 4, 8, BLOCK), F32),
            dma((5,)), dma((5,)), dma((5,)),
            dma((4, 4, 4)), dma((4, 4, 4)), dma((15,)), dma,
            dma((8,)), dma, dma((7,)), dma, dma((15,)), dma((4,)), dma((4,)), dma((4,)),
            dma((7,)), dma, dma((16,)), dma, dma, dma,
        ],
        compiler_params=pltpu.CompilerParams(
            collective_id=1, has_side_effects=True, vmem_limit_bytes=56 * 2**20
        ),
        cost_estimate=pl.CostEstimate(
            flops=2 * PANEL * 1024 * HALF, bytes_accessed=10 * 2**20, transcendentals=0
        ),
        name="panels",
    )(features, prior)


def lane(tile, k):
    return jnp.broadcast_to(tile[:, k : k + 1], (8, 128))


def sublane(tile, k):
    return jnp.broadcast_to(tile[k : k + 1, :], (8, 128))


def pair_sum(terms):
    while len(terms) > 1:
        terms = [terms[2 * i] + terms[2 * i + 1] for i in range(len(terms) // 2)]
    return terms[0]


def inverse_128(tile, between):
    s = [tile[8 * i : 8 * i + 8] for i in range(16)]
    rows = lax.broadcasted_iota(jnp.int32, (8, 128), 0)
    cols = lax.broadcasted_iota(jnp.int32, (8, 128), 1)
    v = [jnp.where(cols == rows + 8 * i, 1.0, 0.0).astype(F32) for i in range(16)]
    out = []

    def collect(parts):
        whole = parts[7]
        for k in range(6, -1, -1):
            whole = jnp.where(rows == k, parts[k], whole)
        return whole

    for p in range(16):
        between(p)
        near = list(range(p, min(16, p + 2)))
        m = [[lane(s[g], 8 * p + k) for k in range(8)] for g in near]
        us, vs = [], []
        for k in range(8):
            inv = lax.rsqrt(sublane(m[0][k], k))
            u, w = sublane(s[p], k) * inv, sublane(v[p], k) * inv
            us.append(u)
            vs.append(w)
            scaled = [sublane(m[0][i], k) * inv for i in range(k + 1, 8)]
            for n, g in enumerate(near):
                if n == 0 and k == 7:
                    continue
                factor = m[n][k] * inv
                for i in range(k + 1, 8):
                    m[n][i] = m[n][i] - factor * scaled[i - k - 1]
                s[g] = s[g] - factor * u
                v[g] = v[g] - factor * w
        out.append(collect(vs))
        if p + 2 < 16:
            turned = collect(us).T
            for i in range(p + 2, 16):
                group = turned[8 * i : 8 * i + 8]
                factors = [lane(group, k) for k in range(8)]
                s[i] = s[i] - pair_sum([f * u for f, u in zip(factors, us)])
                v[i] = v[i] - pair_sum([f * w for f, w in zip(factors, vs)])
    return jnp.concatenate(out, 0)


def dot(left, right):
    return jnp.dot(left, right, precision=lax.Precision.HIGHEST, preferred_element_type=F32)


def dot_t(left, right):
    return lax.dot_general(
        left, right, (((1,), (1,)), ((), ())),
        precision=lax.Precision.HIGHEST, preferred_element_type=F32,
    )


def finish_kernel(panel, other, panel_out, update_out, product, sem):
    panel_copy = pltpu.make_async_copy(panel, panel_out.at[0], sem.at[0])
    panel_copy.start()
    product[...] = jnp.dot(
        panel[...].astype(jnp.bfloat16), other[...], preferred_element_type=F32
    ) * (1.0 / PANEL)
    product_copy = pltpu.make_async_copy(product, update_out.at[0, :, 0, :], sem.at[1])
    product_copy.start()
    panel_copy.wait()
    product_copy.wait()


def on_device(features, prior):
    panel, other = panels(features, prior)
    return pl.pallas_call(
        finish_kernel,
        out_shape=(
            jax.ShapeDtypeStruct((1, PANEL, PANEL), F32),
            jax.ShapeDtypeStruct((1, PANEL, 1, PANEL), F32),
        ),
        in_specs=[pl.BlockSpec(memory_space=pltpu.VMEM)] * 2,
        out_specs=(pl.BlockSpec(memory_space=pl.ANY),) * 2,
        scratch_shapes=[pltpu.VMEM((PANEL, PANEL), F32), pltpu.SemaphoreType.DMA((2,))],
        name="product",
    )(panel, other)


def solution(mesh):
    placed = (P(("row", "col"), None), P())
    return jax.shard_map(
        on_device,
        mesh=mesh,
        in_specs=placed,
        out_specs=(P("row", None, None), P("row", None, "col", None)),
        check_vma=False,
    )
```

```python
import jax
import jax.numpy as jnp
from jax import lax
from jax.experimental import pallas as pl
from jax.experimental.pallas import tpu as pltpu
from jax.sharding import PartitionSpec as P

W = 8192
BLOCK = 256
PANEL = 512
TOKENS = 512
HALF = W // 2
MESH = pl.DeviceIdType.MESH
WIRE = jnp.bfloat16
F32 = jnp.float32
ORDERS = (
    ("xa", "xb", "ya", "yb"),
    ("xb", "ya", "yb", "xa"),
    ("ya", "yb", "xa", "xb"),
    ("yb", "xa", "xb", "ya"),
)
FULL = slice(None)
TOP_WAVES = {3: 1, 5: 2}
LAST_WAVE, END_Z, PASS = (0, 4), (1, 0), (3, 12)


class Place:
    def __init__(self):
        self.r = lax.axis_index("row")
        self.c = lax.axis_index("col")
        self.x = self.r % 4
        self.y = (self.c // 2) % 4
        self.zh = self.r // 4
        self.zl = self.c // 8
        self.z = self.zh * 2 + self.zl
        self.core = self.c % 2
        self.bits = {
            "xa": ((self.x + 1) // 2) % 2,
            "xb": self.x // 2,
            "ya": ((self.y + 1) // 2) % 2,
            "yb": self.y // 2,
        }

    def at(self, x=None, y=None, z=None, core=None):
        x = self.x if x is None else x
        y = self.y if y is None else y
        z = self.z if z is None else z
        core = self.core if core is None else core
        return (z // 2 * 4 + x, z % 2 * 8 + y * 2 + core)

    def partner(self, dim):
        if dim == "xa":
            return self.at(x=self.x + 1 - 2 * (self.x % 2))
        if dim == "xb":
            return self.at(x=3 - self.x)
        if dim == "ya":
            return self.at(y=self.y + 1 - 2 * (self.y % 2))
        return self.at(y=3 - self.y)


def tile_index(place, quarter, zh, step, last):
    fixed = {}
    for k, dim in enumerate(ORDERS[quarter][: step + 1]):
        mine = place.bits[dim]
        fixed[dim] = mine if (k < step or last) else 1 - mine
    pick = lambda dim: fixed.get(dim, FULL)
    return (zh, pick("xb"), pick("xa"), quarter, pick("ya"), pick("yb"))


def strip(y):
    return 2 * (((y + 1) // 2) % 2) + y // 2


def top_slot(x, y):
    return 4 * strip(y) + 2 * (x // 2) + ((x + 1) // 2) % 2


def panel_kernel(feat, prior, panel_out, other, rows_out, top_out, a, g, work, v, below, inv, lead, rest, own, theirs, lead_own, lead_their, lead_t, acc, top, top_parts,
                  s0, s1, s2, s3, r0, r1, r2, r3,
                  zsend, zrecv, zown, topz,
                  load_sem, feat_send, feat_recv, step_send, step_recv, ts_send, ts_recv,
                  z_send, z_recv, tz_send, tz_recv, tg_send, tg_recv, core_send, core_recv,
                  row_send, row_recv, col_send, col_recv, pass_send, pass_recv):
    me = Place()
    sends, recvs = (s0, s1, s2, s3), (r0, r1, r2, r3)
    mate = me.at(core=1 - me.core)
    loads = [pltpu.make_async_copy(feat.at[:, pl.ds(0, PANEL)], lead_own, load_sem.at[0])]
    for i in range(4):
        loads.append(
            pltpu.make_async_copy(
                feat.at[:, pl.ds(pl.multiple_of(me.core * HALF + i * 1024, 1024), 1024)],
                own.at[:, pl.ds(i * 1024, 1024)],
                load_sem.at[i + 1],
            )
        )
    for load in loads:
        load.start()

    barrier = pltpu.get_barrier_semaphore()

    def greet(device):
        pl.semaphore_signal(barrier, inc=1, device_id=device, device_id_type=MESH)

    greet(mate)
    for j in range(1, 16):
        greet(me.at(x=(me.x + j) % 4, y=(me.y + j // 4) % 4))
    for j in range(1, 8):
        greet(me.at(z=(me.z + j) % 8))
    pl.semaphore_wait(barrier, 23)

    shares = [
        pltpu.make_async_remote_copy(
            src_ref=feat.at[:, pl.ds(0, PANEL)], dst_ref=lead_their,
            send_sem=feat_send.at[0], recv_sem=feat_recv.at[0],
            device_id=mate, device_id_type=MESH,
        )
    ]
    for i in range(4):
        shares.append(
            pltpu.make_async_remote_copy(
                src_ref=feat.at[:, pl.ds(pl.multiple_of((1 - me.core) * HALF + i * 1024, 1024), 1024)],
                dst_ref=theirs.at[:, pl.ds(i * 1024, 1024)],
                send_sem=feat_send.at[i + 1], recv_sem=feat_recv.at[i + 1],
                device_id=mate, device_id_type=MESH,
            )
        )
    for share in shares:
        share.start()

    loads[0].wait()
    lead_t[:, :TOKENS] = lead_own[...].T
    shares[0].wait_recv()
    lead_t[:, TOKENS:] = lead_their[...].T

    def products(left, right, rows=FULL):
        return jnp.dot(lead_t[rows, :TOKENS], left, preferred_element_type=F32) + jnp.dot(
            lead_t[rows, TOKENS:], right, preferred_element_type=F32
        )

    lanes = pl.ds(pl.multiple_of(me.core * BLOCK, BLOCK), BLOCK)
    rows = pl.ds(pl.multiple_of(BLOCK + 128 * me.core, 128), 128)
    square = jnp.concatenate(
        [
            products(lead_own[:, lanes], lead_their[:, lanes], lanes),
            products(lead_own[:, :BLOCK], lead_their[:, :BLOCK], rows),
        ],
        0,
    ).reshape(3, 16, 8, BLOCK)
    for t in range(16):
        top[t] = square[:, t]

    def exchange(src, dst, send, recv, device):
        return pltpu.make_async_remote_copy(
            src_ref=src, dst_ref=dst, send_sem=send, recv_sem=recv,
            device_id=device, device_id_type=MESH,
        )

    def main_copy(step, zh, q):
        return exchange(
            sends[step].at[zh, q], recvs[step].at[zh, q],
            step_send.at[step, zh, q], step_recv.at[step, zh, q],
            me.partner(ORDERS[q][step]),
        )

    def main_start(step, zh):
        for q in range(4):
            sends[step][zh, q] = acc[tile_index(me, q, zh, step, False)].astype(WIRE)
            main_copy(step, zh, q).start()

    def main_finish(step, zh):
        for q in range(4):
            main_copy(step, zh, q).wait_recv()
            at = tile_index(me, q, zh, step, True)
            acc[at] = acc[at] + recvs[step][zh, q].astype(F32)

    def multiply(zh):
        loads[zh + 1].wait()
        shares[zh + 1].wait_recv()

        def body(p, carry):
            xb, xa = p // 2, p % 2
            x = 2 * xb + (xb + xa) % 2
            at = pl.ds(pl.multiple_of((zh * 4 + x) * BLOCK, BLOCK), BLOCK)
            acc[zh, xb, xa] = products(own[:, at], theirs[:, at]).reshape(4, 2, 2, 32, BLOCK)
            return carry

        lax.fori_loop(0, 4, body, 0)

    my_slot = top_slot(me.x, me.y)
    plane_at = [((me.x + j) % 4, (me.y + j // 4) % 4) for j in range(1, 16)]
    top_sums = [
        exchange(top.at[top_slot(x, y)], top_parts.at[my_slot], ts_send.at[j], ts_recv, me.at(x=x, y=y))
        for j, (x, y) in enumerate(plane_at)
    ]
    top_column = [
        exchange(topz.at[me.z], topz.at[me.z], tz_send.at[j - 1], tz_recv, me.at(z=(me.z + j) % 8))
        for j in range(1, 8)
    ]
    top_gather = [
        exchange(top_out.at[me.core, my_slot], top_out.at[me.core, my_slot],
                 tg_send.at[j], tg_recv.at[(j + 1) // 4], me.at(x=x, y=y))
        for j, (x, y) in enumerate(plane_at)
    ]
    top_pass = []
    for k in range(4):
        four = top_out.at[me.core, pl.ds(4 * strip((me.y + 4 - k) % 4), 4)]
        top_pass.append(exchange(four, four, core_send.at[k], core_recv.at[k], mate))

    def top_stage(stage):
        if stage == 0:
            for copy in top_sums:
                copy.start()
        if stage == 1:
            fifteen = top_parts.at[pl.ds(0, 15)]
            pltpu.make_async_copy(fifteen, fifteen, ts_recv).wait()
            top_parts[my_slot] = top[my_slot]
            topz[me.z] = pair_sum([top_parts[t] for t in range(16)])
            for copy in top_column:
                copy.start()
        if stage == 2:
            seven = topz.at[pl.ds(0, 7)]
            pltpu.make_async_copy(seven, seven, tz_recv).wait()
            top_out[me.core, my_slot] = pair_sum([topz[z] for z in range(8)])
            for copy in top_gather:
                copy.start()
        if stage == 3:
            for k in range(4):
                some = top_out.at[me.core, pl.ds(0, 4 if k else 3)]
                pltpu.make_async_copy(some, some, tg_recv.at[k]).wait()
                top_pass[k].start()

    home = lambda q, zh: (zh, me.bits["xb"], me.bits["xa"], q, me.bits["ya"], me.bits["yb"])
    column = [exchange(zsend.at[z], zrecv.at[me.z], z_send.at[z], z_recv, me.at(z=z)) for z in range(8)]

    def send_strips(zh):
        for q in range(4):
            tile = acc[home(q, zh)]
            for zl in range(2):
                zsend[zh * 2 + zl, q] = tile[:, zl * 128 : zl * 128 + 128].astype(WIRE)
        for z in (2 * zh, 2 * zh + 1):
            pl.when(me.z != z)(column[z].start)

    def wave(number):
        if number < 4:
            multiply(number)
            main_start(0, number)
        for step in range(4):
            zh = number - step - 1
            if 0 <= zh < 4:
                main_finish(step, zh)
                if step < 3:
                    main_start(step + 1, zh)
                else:
                    send_strips(zh)

    top_stage(0)
    for number in range(7):
        if number in TOP_WAVES:
            top_stage(TOP_WAVES[number])
        wave(number)
    top_stage(3)

    for copy in top_pass:
        copy.wait_recv()
    for h in range(2):
        for q in range(3):
            start, side = ((128 * q, 0), ((384, 0) if q == 2 else (BLOCK + 128 * q, BLOCK)))[h]
            for t in range(16):
                a[pl.ds(start + 8 * t, 8), pl.ds(side, BLOCK)] = top_out[h, t, q]
    for b in range(4):
        at = pl.ds(128 * b, 128)
        i = lax.broadcasted_iota(jnp.int32, (128, 128), 0)
        j = lax.broadcasted_iota(jnp.int32, (128, 128), 1)
        a[at, at] = a[at, at] + jnp.where(i == j, prior[at].reshape(1, 128), 0.0)

    slot = 8 * me.core + 4 * me.zl + 2 * me.bits["ya"] + me.bits["yb"]
    mine = rows_out.at[0, slot]
    row_copies = [
        exchange(mine, mine, row_send.at[j - 1], row_recv,
                 me.at(y=(me.y + j) % 4, z=2 * me.zh + (me.zl + j // 4) % 2))
        for j in range(1, 8)
    ]
    eight = rows_out.at[0, pl.ds(8 * me.core, 8)]
    row_pass = exchange(eight, eight, pass_send, pass_recv, mate)
    col_copies = [
        exchange(mine, rows_out.at[1, slot], col_send.at[j], col_recv, ((me.r + j) % 16, me.r))
        for j in range(16)
    ]

    def last_wave():
        wave(7)

    def finish_z():
        for q in range(4):
            tile = acc[home(q, me.zh)]
            for zl in range(2):
                zown[zl, q] = tile[:, zl * 128 : zl * 128 + 128]
        pltpu.make_async_copy(zrecv.at[pl.ds(0, 7)], zrecv.at[pl.ds(0, 7)], z_recv).wait()
        for q in range(4):
            total = zown[me.zl, q]
            for j in range(1, 8):
                total = total + zrecv[(me.z + j) % 8, q].astype(F32)
            rows_out[0, slot, q] = total.astype(rows_out.dtype)
        for copy in row_copies + col_copies[1:]:
            copy.start()

        @pl.when(me.r != me.c)
        def _():
            col_copies[0].start()

        @pl.when(me.r == me.c)
        def _():
            rows_out[1, slot] = rows_out[0, slot]

    def second_tile(tile):
        below[...] = dot_t(tile[128:BLOCK, :128], v[0])
        work[...] = tile[128:BLOCK, 128:BLOCK] - dot_t(below[...], below[...])

    def finish_inverse(half):
        inv[half, :128, :128] = v[0]
        inv[half, :128, 128:] = jnp.zeros((128, 128), F32)
        inv[half, 128:, :128] = -dot(v[1], dot(below[...], v[0]))
        inv[half, 128:, 128:] = v[1]

    def pass_rows():
        seven = rows_out.at[0, pl.ds(0, 7)]
        pltpu.make_async_copy(seven, seven, row_recv).wait()
        row_pass.start()

    def factorise(b, carry):
        @pl.when(b == 0)
        def _():
            work[...] = a[:128, :128]

        @pl.when(b == 1)
        def _():
            second_tile(a)

        @pl.when(b == 2)
        def _():
            finish_inverse(0)
            lead[...] = dot_t(a[BLOCK:, :BLOCK], inv[0])
            rest[...] = a[BLOCK:, BLOCK:] - dot_t(lead[...], lead[...])
            work[...] = rest[:128, :128]

        @pl.when(b == 3)
        def _():
            second_tile(rest)

        def between(panel):
            for when, act in ((LAST_WAVE, last_wave), (END_Z, finish_z), (PASS, pass_rows)):
                if panel == when[1]:
                    pl.when(b == when[0])(act)

        v[b % 2] = inverse_128(work[...], between)
        return carry

    lax.fori_loop(0, 4, factorise, 0)
    finish_inverse(1)

    def assemble(side):
        for h in range(2):
            for zl in range(2):
                for t in range(4):
                    for q in range(4):
                        g[side, pl.ds(128 * q + 32 * t, 32), pl.ds(BLOCK * h + 128 * zl, 128)] = (
                            rows_out[side, 8 * h + 4 * zl + t, q].astype(F32)
                        )
        for b in range(2):

            @pl.when((me.r, me.c)[side] == b)
            def _():
                g[side, :BLOCK, :BLOCK] = a[BLOCK:, :BLOCK].T if b else a[:BLOCK, :BLOCK]
                g[side, BLOCK:, :BLOCK] = a[BLOCK:, pl.ds(BLOCK * b, BLOCK)]

    row_pass.wait_recv()
    assemble(0)
    for b in range(2):
        at = pl.ds(BLOCK * b, BLOCK)
        first = dot_t(g[0, :BLOCK, at].T, inv[0])
        second = dot_t(g[0, BLOCK:, at].T - dot_t(first, lead[...]), inv[1])
        if b == 0:
            second = jnp.where(me.r == 0, 0.0, second)
        panel_out[at, :BLOCK] = first
        panel_out[at, BLOCK:] = second

    @pl.when(me.r != me.c)
    def _():
        pltpu.make_async_copy(rows_out.at[1], rows_out.at[1], col_recv).wait()
        col_copies[0].wait_send()

    @pl.when(me.r == me.c)
    def _():
        fifteen = rows_out.at[1, pl.ds(0, 15)]
        pltpu.make_async_copy(fifteen, fifteen, col_recv).wait()

    assemble(1)
    first = dot(inv[0], g[1, :BLOCK])
    second = dot(inv[1], g[1, BLOCK:] - dot(lead[...], first))
    other[:BLOCK] = first.astype(jnp.bfloat16)
    other[BLOCK:, :BLOCK] = jnp.where(me.c == 0, 0.0, second[:, :BLOCK]).astype(jnp.bfloat16)
    other[BLOCK:, BLOCK:] = second[:, BLOCK:].astype(jnp.bfloat16)

    for copies in (row_copies, col_copies[1:], shares, [row_pass]):
        for copy in copies:
            copy.wait_send()
    for z in range(8):
        pl.when(me.z != z)(column[z].wait_send)
    for copies in (top_sums, top_column, top_gather, top_pass):
        for copy in copies:
            copy.wait_send()
    for step in range(4):
        for q in range(4):
            for zh in range(4):
                main_copy(step, zh, q).wait_send()


def panels(features, prior):
    twos = lambda n: (2,) * n
    wire = lambda n: pltpu.VMEM((4, 4) + twos(n) + (32, BLOCK), WIRE)
    dma = pltpu.SemaphoreType.DMA
    return pl.pallas_call(
        panel_kernel,
        out_shape=(
            jax.ShapeDtypeStruct((PANEL, PANEL), F32),
            jax.ShapeDtypeStruct((PANEL, PANEL), jnp.bfloat16),
        ),
        in_specs=[pl.BlockSpec(memory_space=pl.ANY), pl.BlockSpec(memory_space=pltpu.VMEM)],
        out_specs=(pl.BlockSpec(memory_space=pltpu.VMEM),) * 2,
        scratch_shapes=[
            pltpu.VMEM((2, 16, 4, 32, 128), WIRE),
            pltpu.VMEM((2, 16, 3, 8, BLOCK), F32),
            pltpu.VMEM((PANEL, PANEL), F32),
            pltpu.VMEM((2, PANEL, PANEL), F32),
            pltpu.VMEM((128, 128), F32),
            pltpu.VMEM((2, 128, 128), F32),
            pltpu.VMEM((128, 128), F32),
            pltpu.VMEM((2, BLOCK, BLOCK), F32),
            pltpu.VMEM((BLOCK, BLOCK), F32),
            pltpu.VMEM((BLOCK, BLOCK), F32),
            pltpu.VMEM((TOKENS, HALF), jnp.bfloat16),
            pltpu.VMEM((TOKENS, HALF), jnp.bfloat16),
            pltpu.VMEM((TOKENS, PANEL), jnp.bfloat16),
            pltpu.VMEM((TOKENS, PANEL), jnp.bfloat16),
            pltpu.VMEM((PANEL, 2 * TOKENS), jnp.bfloat16),
            pltpu.VMEM((4, 2, 2, 4, 2, 2, 32, BLOCK), F32),
            pltpu.VMEM((16, 3, 8, BLOCK), F32),
            pltpu.VMEM((16, 3, 8, BLOCK), F32),
            *[wire(n) for n in (3, 2, 1, 0)],
            *[wire(n) for n in (3, 2, 1, 0)],
            pltpu.VMEM((8, 4, 32, 128), WIRE),
            pltpu.VMEM((8, 4, 32, 128), WIRE),
            pltpu.VMEM((2, 4, 32, 128), F32),
            pltpu.VMEM((8, 3, 8, BLOCK), F32),
            dma((5,)), dma((5,)), dma((5,)),
            dma((4, 4, 4)), dma((4, 4, 4)), dma((15,)), dma,
            dma((8,)), dma, dma((7,)), dma, dma((15,)), dma((4,)), dma((4,)), dma((4,)),
            dma((7,)), dma, dma((16,)), dma, dma, dma,
        ],
        compiler_params=pltpu.CompilerParams(
            collective_id=1, has_side_effects=True, vmem_limit_bytes=56 * 2**20
        ),
        cost_estimate=pl.CostEstimate(
            flops=2 * PANEL * 1024 * HALF, bytes_accessed=10 * 2**20, transcendentals=0
        ),
        name="panels",
    )(features, prior)


def lane(tile, k):
    return jnp.broadcast_to(tile[:, k : k + 1], (8, 128))


def sublane(tile, k):
    return jnp.broadcast_to(tile[k : k + 1, :], (8, 128))


def pair_sum(terms):
    while len(terms) > 1:
        terms = [terms[2 * i] + terms[2 * i + 1] for i in range(len(terms) // 2)]
    return terms[0]


def inverse_128(tile, between):
    s = [tile[8 * i : 8 * i + 8] for i in range(16)]
    rows = lax.broadcasted_iota(jnp.int32, (8, 128), 0)
    cols = lax.broadcasted_iota(jnp.int32, (8, 128), 1)
    v = [jnp.where(cols == rows + 8 * i, 1.0, 0.0).astype(F32) for i in range(16)]
    out = []

    def collect(parts):
        whole = parts[7]
        for k in range(6, -1, -1):
            whole = jnp.where(rows == k, parts[k], whole)
        return whole

    for p in range(16):
        between(p)
        near = list(range(p, min(16, p + 2)))
        m = [[lane(s[g], 8 * p + k) for k in range(8)] for g in near]
        us, vs = [], []
        for k in range(8):
            inv = lax.rsqrt(sublane(m[0][k], k))
            u, w = sublane(s[p], k) * inv, sublane(v[p], k) * inv
            us.append(u)
            vs.append(w)
            scaled = [sublane(m[0][i], k) * inv for i in range(k + 1, 8)]
            for n, g in enumerate(near):
                if n == 0 and k == 7:
                    continue
                factor = m[n][k] * inv
                for i in range(k + 1, 8):
                    m[n][i] = m[n][i] - factor * scaled[i - k - 1]
                s[g] = s[g] - factor * u
                v[g] = v[g] - factor * w
        out.append(collect(vs))
        if p + 2 < 16:
            turned = collect(us).T
            for i in range(p + 2, 16):
                group = turned[8 * i : 8 * i + 8]
                factors = [lane(group, k) for k in range(8)]
                s[i] = s[i] - pair_sum([f * u for f, u in zip(factors, us)])
                v[i] = v[i] - pair_sum([f * w for f, w in zip(factors, vs)])
    return jnp.concatenate(out, 0)


def dot(left, right):
    return jnp.dot(left, right, precision=lax.Precision.HIGHEST, preferred_element_type=F32)


def dot_t(left, right):
    return lax.dot_general(
        left, right, (((1,), (1,)), ((), ())),
        precision=lax.Precision.HIGHEST, preferred_element_type=F32,
    )


def finish_kernel(panel, other, panel_out, update_out, product, sem):
    panel_copy = pltpu.make_async_copy(panel, panel_out.at[0], sem.at[0])
    panel_copy.start()
    product[...] = jnp.dot(
        panel[...].astype(jnp.bfloat16), other[...], preferred_element_type=F32
    ) * (1.0 / PANEL)
    product_copy = pltpu.make_async_copy(product, update_out.at[0, :, 0, :], sem.at[1])
    product_copy.start()
    panel_copy.wait()
    product_copy.wait()


def on_device(features, prior):
    panel, other = panels(features, prior)
    return pl.pallas_call(
        finish_kernel,
        out_shape=(
            jax.ShapeDtypeStruct((1, PANEL, PANEL), F32),
            jax.ShapeDtypeStruct((1, PANEL, 1, PANEL), F32),
        ),
        in_specs=[pl.BlockSpec(memory_space=pltpu.VMEM)] * 2,
        out_specs=(pl.BlockSpec(memory_space=pl.ANY),) * 2,
        scratch_shapes=[pltpu.VMEM((PANEL, PANEL), F32), pltpu.SemaphoreType.DMA((2,))],
        name="product",
    )(panel, other)


def solution(mesh):
    placed = (P(("row", "col"), None), P())
    return jax.shard_map(
        on_device,
        mesh=mesh,
        in_specs=placed,
        out_specs=(P("row", None, None), P("row", None, "col", None)),
        check_vma=False,
    )
```

```python
import jax
import jax.numpy as jnp
from jax import lax
from jax.experimental import pallas as pl
from jax.experimental.pallas import tpu as pltpu
from jax.sharding import PartitionSpec as P

W = 8192
BLOCK = 256
PANEL = 512
TOKENS = 512
HALF = W // 2
MESH = pl.DeviceIdType.MESH
WIRE = jnp.bfloat16
F32 = jnp.float32
ORDERS = (
    ("xa", "xb", "ya", "yb"),
    ("xb", "ya", "yb", "xa"),
    ("ya", "yb", "xa", "xb"),
    ("yb", "xa", "xb", "ya"),
)
FULL = slice(None)
TOP_WAVES = {3: 1, 5: 2}
LAST_WAVE, END_Z, PASS = (0, 4), (1, 0), (3, 12)


class Place:
    def __init__(self):
        self.r = lax.axis_index("row")
        self.c = lax.axis_index("col")
        self.x = self.r % 4
        self.y = (self.c // 2) % 4
        self.zh = self.r // 4
        self.zl = self.c // 8
        self.z = self.zh * 2 + self.zl
        self.core = self.c % 2
        self.bits = {
            "xa": ((self.x + 1) // 2) % 2,
            "xb": self.x // 2,
            "ya": ((self.y + 1) // 2) % 2,
            "yb": self.y // 2,
        }

    def at(self, x=None, y=None, z=None, core=None):
        x = self.x if x is None else x
        y = self.y if y is None else y
        z = self.z if z is None else z
        core = self.core if core is None else core
        return (z // 2 * 4 + x, z % 2 * 8 + y * 2 + core)

    def partner(self, dim):
        if dim == "xa":
            return self.at(x=self.x + 1 - 2 * (self.x % 2))
        if dim == "xb":
            return self.at(x=3 - self.x)
        if dim == "ya":
            return self.at(y=self.y + 1 - 2 * (self.y % 2))
        return self.at(y=3 - self.y)


def tile_index(place, quarter, zh, step, last):
    fixed = {}
    for k, dim in enumerate(ORDERS[quarter][: step + 1]):
        mine = place.bits[dim]
        fixed[dim] = mine if (k < step or last) else 1 - mine
    pick = lambda dim: fixed.get(dim, FULL)
    return (zh, pick("xb"), pick("xa"), quarter, pick("ya"), pick("yb"))


def strip(y):
    return 2 * (((y + 1) // 2) % 2) + y // 2


def top_slot(x, y):
    return 4 * strip(y) + 2 * (x // 2) + ((x + 1) // 2) % 2


def panel_kernel(feat, prior, panel_out, other, rows_out, top_out, a, g, work, v, below, inv, lead, rest, own, theirs, lead_own, lead_their, lead_t, acc, top, top_parts,
                  s0, s1, s2, s3, r0, r1, r2, r3,
                  zsend, zrecv, zown, topz,
                  load_sem, feat_send, feat_recv, step_send, step_recv, ts_send, ts_recv,
                  z_send, z_recv, tz_send, tz_recv, tg_send, tg_recv, core_send, core_recv,
                  row_send, row_recv, col_send, col_recv, pass_send, pass_recv):
    me = Place()
    sends, recvs = (s0, s1, s2, s3), (r0, r1, r2, r3)
    mate = me.at(core=1 - me.core)
    loads = [pltpu.make_async_copy(feat.at[:, pl.ds(0, PANEL)], lead_own, load_sem.at[0])]
    for i in range(4):
        loads.append(
            pltpu.make_async_copy(
                feat.at[:, pl.ds(pl.multiple_of(me.core * HALF + i * 1024, 1024), 1024)],
                own.at[:, pl.ds(i * 1024, 1024)],
                load_sem.at[i + 1],
            )
        )
    for load in loads:
        load.start()

    barrier = pltpu.get_barrier_semaphore()

    def greet(device):
        pl.semaphore_signal(barrier, inc=1, device_id=device, device_id_type=MESH)

    greet(mate)
    for j in range(1, 16):
        greet(me.at(x=(me.x + j) % 4, y=(me.y + j // 4) % 4))
    for j in range(1, 8):
        greet(me.at(z=(me.z + j) % 8))
    pl.semaphore_wait(barrier, 23)

    shares = [
        pltpu.make_async_remote_copy(
            src_ref=feat.at[:, pl.ds(0, PANEL)], dst_ref=lead_their,
            send_sem=feat_send.at[0], recv_sem=feat_recv.at[0],
            device_id=mate, device_id_type=MESH,
        )
    ]
    for i in range(4):
        shares.append(
            pltpu.make_async_remote_copy(
                src_ref=feat.at[:, pl.ds(pl.multiple_of((1 - me.core) * HALF + i * 1024, 1024), 1024)],
                dst_ref=theirs.at[:, pl.ds(i * 1024, 1024)],
                send_sem=feat_send.at[i + 1], recv_sem=feat_recv.at[i + 1],
                device_id=mate, device_id_type=MESH,
            )
        )
    for share in shares:
        share.start()

    loads[0].wait()
    lead_t[:, :TOKENS] = lead_own[...].T
    shares[0].wait_recv()
    lead_t[:, TOKENS:] = lead_their[...].T

    def products(left, right, rows=FULL):
        return jnp.dot(lead_t[rows, :TOKENS], left, preferred_element_type=F32) + jnp.dot(
            lead_t[rows, TOKENS:], right, preferred_element_type=F32
        )

    lanes = pl.ds(pl.multiple_of(me.core * BLOCK, BLOCK), BLOCK)
    rows = pl.ds(pl.multiple_of(BLOCK + 128 * me.core, 128), 128)
    square = jnp.concatenate(
        [
            products(lead_own[:, lanes], lead_their[:, lanes], lanes),
            products(lead_own[:, :BLOCK], lead_their[:, :BLOCK], rows),
        ],
        0,
    ).reshape(3, 16, 8, BLOCK)
    for t in range(16):
        top[t] = square[:, t]

    def exchange(src, dst, send, recv, device):
        return pltpu.make_async_remote_copy(
            src_ref=src, dst_ref=dst, send_sem=send, recv_sem=recv,
            device_id=device, device_id_type=MESH,
        )

    def main_copy(step, zh, q):
        return exchange(
            sends[step].at[zh, q], recvs[step].at[zh, q],
            step_send.at[step, zh, q], step_recv.at[step, zh, q],
            me.partner(ORDERS[q][step]),
        )

    def main_start(step, zh):
        for q in range(4):
            sends[step][zh, q] = acc[tile_index(me, q, zh, step, False)].astype(WIRE)
            main_copy(step, zh, q).start()

    def main_finish(step, zh):
        for q in range(4):
            main_copy(step, zh, q).wait_recv()
            at = tile_index(me, q, zh, step, True)
            acc[at] = acc[at] + recvs[step][zh, q].astype(F32)

    def multiply(zh):
        loads[zh + 1].wait()
        shares[zh + 1].wait_recv()

        def body(p, carry):
            xb, xa = p // 2, p % 2
            x = 2 * xb + (xb + xa) % 2
            at = pl.ds(pl.multiple_of((zh * 4 + x) * BLOCK, BLOCK), BLOCK)
            acc[zh, xb, xa] = products(own[:, at], theirs[:, at]).reshape(4, 2, 2, 32, BLOCK)
            return carry

        lax.fori_loop(0, 4, body, 0)

    my_slot = top_slot(me.x, me.y)
    plane_at = [((me.x + j) % 4, (me.y + j // 4) % 4) for j in range(1, 16)]
    top_sums = [
        exchange(top.at[top_slot(x, y)], top_parts.at[my_slot], ts_send.at[j], ts_recv, me.at(x=x, y=y))
        for j, (x, y) in enumerate(plane_at)
    ]
    top_column = [
        exchange(topz.at[me.z], topz.at[me.z], tz_send.at[j - 1], tz_recv, me.at(z=(me.z + j) % 8))
        for j in range(1, 8)
    ]
    top_gather = [
        exchange(top_out.at[me.core, my_slot], top_out.at[me.core, my_slot],
                 tg_send.at[j], tg_recv.at[(j + 1) // 4], me.at(x=x, y=y))
        for j, (x, y) in enumerate(plane_at)
    ]
    top_pass = []
    for k in range(4):
        four = top_out.at[me.core, pl.ds(4 * strip((me.y + 4 - k) % 4), 4)]
        top_pass.append(exchange(four, four, core_send.at[k], core_recv.at[k], mate))

    def top_stage(stage):
        if stage == 0:
            for copy in top_sums:
                copy.start()
        if stage == 1:
            fifteen = top_parts.at[pl.ds(0, 15)]
            pltpu.make_async_copy(fifteen, fifteen, ts_recv).wait()
            top_parts[my_slot] = top[my_slot]
            topz[me.z] = pair_sum([top_parts[t] for t in range(16)])
            for copy in top_column:
                copy.start()
        if stage == 2:
            seven = topz.at[pl.ds(0, 7)]
            pltpu.make_async_copy(seven, seven, tz_recv).wait()
            top_out[me.core, my_slot] = pair_sum([topz[z] for z in range(8)])
            for copy in top_gather:
                copy.start()
        if stage == 3:
            for k in range(4):
                some = top_out.at[me.core, pl.ds(0, 4 if k else 3)]
                pltpu.make_async_copy(some, some, tg_recv.at[k]).wait()
                top_pass[k].start()

    home = lambda q, zh: (zh, me.bits["xb"], me.bits["xa"], q, me.bits["ya"], me.bits["yb"])
    column = [exchange(zsend.at[z], zrecv.at[me.z], z_send.at[z], z_recv, me.at(z=z)) for z in range(8)]

    def send_strips(zh):
        for q in range(4):
            tile = acc[home(q, zh)]
            for zl in range(2):
                zsend[zh * 2 + zl, q] = tile[:, zl * 128 : zl * 128 + 128].astype(WIRE)
        for z in (2 * zh, 2 * zh + 1):
            pl.when(me.z != z)(column[z].start)

    def wave(number):
        if number < 4:
            multiply(number)
            main_start(0, number)
        for step in range(4):
            zh = number - step - 1
            if 0 <= zh < 4:
                main_finish(step, zh)
                if step < 3:
                    main_start(step + 1, zh)
                else:
                    send_strips(zh)

    top_stage(0)
    for number in range(7):
        if number in TOP_WAVES:
            top_stage(TOP_WAVES[number])
        wave(number)
    top_stage(3)

    for copy in top_pass:
        copy.wait_recv()
    for h in range(2):
        for q in range(3):
            start, side = ((128 * q, 0), ((384, 0) if q == 2 else (BLOCK + 128 * q, BLOCK)))[h]
            for t in range(16):
                a[pl.ds(start + 8 * t, 8), pl.ds(side, BLOCK)] = top_out[h, t, q]
    for b in range(4):
        at = pl.ds(128 * b, 128)
        i = lax.broadcasted_iota(jnp.int32, (128, 128), 0)
        j = lax.broadcasted_iota(jnp.int32, (128, 128), 1)
        a[at, at] = a[at, at] + jnp.where(i == j, prior[at].reshape(1, 128), 0.0)

    slot = 8 * me.core + 4 * me.zl + 2 * me.bits["ya"] + me.bits["yb"]
    mine = rows_out.at[0, slot]
    row_copies = [
        exchange(mine, mine, row_send.at[j - 1], row_recv,
                 me.at(y=(me.y + j) % 4, z=2 * me.zh + (me.zl + j // 4) % 2))
        for j in range(1, 8)
    ]
    eight = rows_out.at[0, pl.ds(8 * me.core, 8)]
    row_pass = exchange(eight, eight, pass_send, pass_recv, mate)
    col_copies = [
        exchange(mine, rows_out.at[1, slot], col_send.at[j], col_recv, ((me.r + j) % 16, me.r))
        for j in range(16)
    ]

    def last_wave():
        wave(7)

    def finish_z():
        for q in range(4):
            tile = acc[home(q, me.zh)]
            for zl in range(2):
                zown[zl, q] = tile[:, zl * 128 : zl * 128 + 128]
        pltpu.make_async_copy(zrecv.at[pl.ds(0, 7)], zrecv.at[pl.ds(0, 7)], z_recv).wait()
        for q in range(4):
            total = zown[me.zl, q]
            for j in range(1, 8):
                total = total + zrecv[(me.z + j) % 8, q].astype(F32)
            rows_out[0, slot, q] = total.astype(rows_out.dtype)
        for copy in row_copies + col_copies[1:]:
            copy.start()

        @pl.when(me.r != me.c)
        def _():
            col_copies[0].start()

        @pl.when(me.r == me.c)
        def _():
            rows_out[1, slot] = rows_out[0, slot]

    def second_tile(tile):
        below[...] = dot_t(tile[128:BLOCK, :128], v[0])
        work[...] = tile[128:BLOCK, 128:BLOCK] - dot_t(below[...], below[...])

    def finish_inverse(half):
        inv[half, :128, :128] = v[0]
        inv[half, :128, 128:] = jnp.zeros((128, 128), F32)
        inv[half, 128:, :128] = -dot(v[1], dot(below[...], v[0]))
        inv[half, 128:, 128:] = v[1]

    def pass_rows():
        seven = rows_out.at[0, pl.ds(0, 7)]
        pltpu.make_async_copy(seven, seven, row_recv).wait()
        row_pass.start()

    def factorise(b, carry):
        @pl.when(b == 0)
        def _():
            work[...] = a[:128, :128]

        @pl.when(b == 1)
        def _():
            second_tile(a)

        @pl.when(b == 2)
        def _():
            finish_inverse(0)
            lead[...] = dot_t(a[BLOCK:, :BLOCK], inv[0])
            rest[...] = a[BLOCK:, BLOCK:] - dot_t(lead[...], lead[...])
            work[...] = rest[:128, :128]

        @pl.when(b == 3)
        def _():
            second_tile(rest)

        def between(panel):
            for when, act in ((LAST_WAVE, last_wave), (END_Z, finish_z), (PASS, pass_rows)):
                if panel == when[1]:
                    pl.when(b == when[0])(act)

        v[b % 2] = inverse_128(work[...], between)
        return carry

    lax.fori_loop(0, 4, factorise, 0)
    finish_inverse(1)

    def assemble(side):
        for h in range(2):
            for zl in range(2):
                for t in range(4):
                    for q in range(4):
                        g[side, pl.ds(128 * q + 32 * t, 32), pl.ds(BLOCK * h + 128 * zl, 128)] = (
                            rows_out[side, 8 * h + 4 * zl + t, q].astype(F32)
                        )
        for b in range(2):

            @pl.when((me.r, me.c)[side] == b)
            def _():
                g[side, :BLOCK, :BLOCK] = a[BLOCK:, :BLOCK].T if b else a[:BLOCK, :BLOCK]
                g[side, BLOCK:, :BLOCK] = a[BLOCK:, pl.ds(BLOCK * b, BLOCK)]

    row_pass.wait_recv()
    assemble(0)
    for b in range(2):
        at = pl.ds(BLOCK * b, BLOCK)
        first = dot_t(g[0, :BLOCK, at].T, inv[0])
        second = dot_t(g[0, BLOCK:, at].T - dot_t(first, lead[...]), inv[1])
        if b == 0:
            second = jnp.where(me.r == 0, 0.0, second)
        panel_out[at, :BLOCK] = first
        panel_out[at, BLOCK:] = second

    @pl.when(me.r != me.c)
    def _():
        pltpu.make_async_copy(rows_out.at[1], rows_out.at[1], col_recv).wait()
        col_copies[0].wait_send()

    @pl.when(me.r == me.c)
    def _():
        fifteen = rows_out.at[1, pl.ds(0, 15)]
        pltpu.make_async_copy(fifteen, fifteen, col_recv).wait()

    assemble(1)
    first = dot(inv[0], g[1, :BLOCK])
    second = dot(inv[1], g[1, BLOCK:] - dot(lead[...], first))
    other[:BLOCK] = first.astype(jnp.bfloat16)
    other[BLOCK:, :BLOCK] = jnp.where(me.c == 0, 0.0, second[:, :BLOCK]).astype(jnp.bfloat16)
    other[BLOCK:, BLOCK:] = second[:, BLOCK:].astype(jnp.bfloat16)

    for copies in (row_copies, col_copies[1:], shares, [row_pass]):
        for copy in copies:
            copy.wait_send()
    for z in range(8):
        pl.when(me.z != z)(column[z].wait_send)
    for copies in (top_sums, top_column, top_gather, top_pass):
        for copy in copies:
            copy.wait_send()
    for step in range(4):
        for q in range(4):
            for zh in range(4):
                main_copy(step, zh, q).wait_send()


def panels(features, prior):
    twos = lambda n: (2,) * n
    wire = lambda n: pltpu.VMEM((4, 4) + twos(n) + (32, BLOCK), WIRE)
    dma = pltpu.SemaphoreType.DMA
    return pl.pallas_call(
        panel_kernel,
        out_shape=(
            jax.ShapeDtypeStruct((PANEL, PANEL), F32),
            jax.ShapeDtypeStruct((PANEL, PANEL), jnp.bfloat16),
        ),
        in_specs=[pl.BlockSpec(memory_space=pl.ANY), pl.BlockSpec(memory_space=pltpu.VMEM)],
        out_specs=(pl.BlockSpec(memory_space=pltpu.VMEM),) * 2,
        scratch_shapes=[
            pltpu.VMEM((2, 16, 4, 32, 128), WIRE),
            pltpu.VMEM((2, 16, 3, 8, BLOCK), F32),
            pltpu.VMEM((PANEL, PANEL), F32),
            pltpu.VMEM((2, PANEL, PANEL), F32),
            pltpu.VMEM((128, 128), F32),
            pltpu.VMEM((2, 128, 128), F32),
            pltpu.VMEM((128, 128), F32),
            pltpu.VMEM((2, BLOCK, BLOCK), F32),
            pltpu.VMEM((BLOCK, BLOCK), F32),
            pltpu.VMEM((BLOCK, BLOCK), F32),
            pltpu.VMEM((TOKENS, HALF), jnp.bfloat16),
            pltpu.VMEM((TOKENS, HALF), jnp.bfloat16),
            pltpu.VMEM((TOKENS, PANEL), jnp.bfloat16),
            pltpu.VMEM((TOKENS, PANEL), jnp.bfloat16),
            pltpu.VMEM((PANEL, 2 * TOKENS), jnp.bfloat16),
            pltpu.VMEM((4, 2, 2, 4, 2, 2, 32, BLOCK), F32),
            pltpu.VMEM((16, 3, 8, BLOCK), F32),
            pltpu.VMEM((16, 3, 8, BLOCK), F32),
            *[wire(n) for n in (3, 2, 1, 0)],
            *[wire(n) for n in (3, 2, 1, 0)],
            pltpu.VMEM((8, 4, 32, 128), WIRE),
            pltpu.VMEM((8, 4, 32, 128), WIRE),
            pltpu.VMEM((2, 4, 32, 128), F32),
            pltpu.VMEM((8, 3, 8, BLOCK), F32),
            dma((5,)), dma((5,)), dma((5,)),
            dma((4, 4, 4)), dma((4, 4, 4)), dma((15,)), dma,
            dma((8,)), dma, dma((7,)), dma, dma((15,)), dma((4,)), dma((4,)), dma((4,)),
            dma((7,)), dma, dma((16,)), dma, dma, dma,
        ],
        compiler_params=pltpu.CompilerParams(
            collective_id=1, has_side_effects=True, vmem_limit_bytes=56 * 2**20
        ),
        cost_estimate=pl.CostEstimate(
            flops=2 * PANEL * 1024 * HALF, bytes_accessed=10 * 2**20, transcendentals=0
        ),
        name="panels",
    )(features, prior)


def lane(tile, k):
    return jnp.broadcast_to(tile[:, k : k + 1], (8, 128))


def sublane(tile, k):
    return jnp.broadcast_to(tile[k : k + 1, :], (8, 128))


def pair_sum(terms):
    while len(terms) > 1:
        terms = [terms[2 * i] + terms[2 * i + 1] for i in range(len(terms) // 2)]
    return terms[0]


def inverse_128(tile, between):
    s = [tile[8 * i : 8 * i + 8] for i in range(16)]
    rows = lax.broadcasted_iota(jnp.int32, (8, 128), 0)
    cols = lax.broadcasted_iota(jnp.int32, (8, 128), 1)
    v = [jnp.where(cols == rows + 8 * i, 1.0, 0.0).astype(F32) for i in range(16)]
    out = []

    def collect(parts):
        whole = parts[7]
        for k in range(6, -1, -1):
            whole = jnp.where(rows == k, parts[k], whole)
        return whole

    for p in range(16):
        between(p)
        near = list(range(p, min(16, p + 2)))
        m = [[lane(s[g], 8 * p + k) for k in range(8)] for g in near]
        us, vs = [], []
        for k in range(8):
            inv = lax.rsqrt(sublane(m[0][k], k))
            u, w = sublane(s[p], k) * inv, sublane(v[p], k) * inv
            us.append(u)
            vs.append(w)
            scaled = [sublane(m[0][i], k) * inv for i in range(k + 1, 8)]
            for n, g in enumerate(near):
                if n == 0 and k == 7:
                    continue
                factor = m[n][k] * inv
                for i in range(k + 1, 8):
                    m[n][i] = m[n][i] - factor * scaled[i - k - 1]
                s[g] = s[g] - factor * u
                v[g] = v[g] - factor * w
        out.append(collect(vs))
        if p + 2 < 16:
            turned = collect(us).T
            for i in range(p + 2, 16):
                group = turned[8 * i : 8 * i + 8]
                factors = [lane(group, k) for k in range(8)]
                s[i] = s[i] - pair_sum([f * u for f, u in zip(factors, us)])
                v[i] = v[i] - pair_sum([f * w for f, w in zip(factors, vs)])
    return jnp.concatenate(out, 0)


def dot(left, right):
    return jnp.dot(left, right, precision=lax.Precision.HIGHEST, preferred_element_type=F32)


def dot_t(left, right):
    return lax.dot_general(
        left, right, (((1,), (1,)), ((), ())),
        precision=lax.Precision.HIGHEST, preferred_element_type=F32,
    )


def finish_kernel(panel, other, panel_out, update_out, left, right, product, sem):
    strips = [pl.ds(128 * i, 128) for i in range(4)]
    load = pltpu.make_async_copy(other, right, sem.at[0])
    load.start()
    loads = [
        pltpu.make_async_copy(panel.at[at], left.at[at], sem.at[1 + i]) for i, at in enumerate(strips)
    ]
    for copy in loads:
        copy.start()
    load.wait()
    stores = []
    for i, at in enumerate(strips):
        loads[i].wait()
        stores.append(pltpu.make_async_copy(left.at[at], panel_out.at[0, at], sem.at[5 + i]))
        stores[-1].start()
        product[at] = jnp.dot(
            left[at].astype(jnp.bfloat16), right[...], preferred_element_type=F32
        ) * (1.0 / PANEL)
        stores.append(
            pltpu.make_async_copy(product.at[at], update_out.at[0, at, 0, :], sem.at[9 + i])
        )
        stores[-1].start()
    for copy in stores:
        copy.wait()


def on_device(features, prior):
    panel, other = panels(features, prior)
    return pl.pallas_call(
        finish_kernel,
        out_shape=(
            jax.ShapeDtypeStruct((1, PANEL, PANEL), F32),
            jax.ShapeDtypeStruct((1, PANEL, 1, PANEL), F32),
        ),
        in_specs=[pl.BlockSpec(memory_space=pl.ANY)] * 2,
        out_specs=(pl.BlockSpec(memory_space=pl.ANY),) * 2,
        scratch_shapes=[
            pltpu.VMEM((PANEL, PANEL), F32),
            pltpu.VMEM((PANEL, PANEL), jnp.bfloat16),
            pltpu.VMEM((PANEL, PANEL), F32),
            pltpu.SemaphoreType.DMA((13,)),
        ],
        name="product",
    )(panel, other)


def solution(mesh):
    placed = (P(("row", "col"), None), P())
    return jax.shard_map(
        on_device,
        mesh=mesh,
        in_specs=placed,
        out_specs=(P("row", None, None), P("row", None, "col", None)),
        check_vma=False,
    )
```
